128 devices in a mesh: gx: 16 (over x, y), gy: 8 (over z, core).
Axes of the slice: x: 4, y: 4, z: 4, core: 2. Of those that a mesh axis runs over, the one named last changes fastest.
Arguments:
- features: bfloat16 [1024, 32, 512], P(('gx', 'gy')), may hold values from -6 to 6
- w_fine: bfloat16 [32, 864], replicated, may hold values from -0.21875 to 0.21875
- w_coarse: bfloat16 [64, 864], replicated, may hold values from -0.625 to 0.625
- w_up: bfloat16 [32, 64], replicated, may hold values from -0.75 to 0.75
- cotangent: bfloat16 [1024, 32, 512], P(('gx', 'gy')), may hold values from -6 to 6
- adjacency: int32 [1024, 27], P(('gx', 'gy')), may hold values from -1 to 1023, as said below
- parents: int32 [1024], P(('gx', 'gy')), may hold values from -1 to 2047, as said below
Outputs:
- layer_out: bfloat16 [1024, 32, 512], P(('gx', 'gy'))
- grad_features: bfloat16 [1024, 32, 512], P(('gx', 'gy'))
- grad_fine: float32 [32, 864], replicated
- grad_coarse: float32 [64, 864], replicated
- grad_up: float32 [32, 64], replicated
The draws below stay inside these ranges and needn't reach their ends.
Inputs may be any that keep to these rules, and one draw needn't show every extreme that they name: `adjacency`: fine slots are numbered device by device in gx+gy order, 8 a device; slot (x * 2 + y) * 2 + k of the device at gx index i and gy index j lies in lattice column (i * 2 + x, j * 2 + y) at one of 4 depths, live slots of a column in rising depth. Row s holds, at ((dx + 1) * 3 + dy + 1) * 3 + dz + 1, the live slot at that lattice offset from s or -1; entry 13 is s when s is live; a slot that is not live has -1 everywhere. Each column has 1 to 2 live slots; the first column holds one; the last device's columns are all full, and the last column's top depth is live. `parents`: -1 for slots that are not live, else 8 q + (ox * 2 + oy) * 2 + oz: the slot at lattice position (X, Y, Z) lies in octant (X % 2, Y % 2, Z % 2) of coarse brick (X / 2, Y / 2, Z / 2) rounded down; coarse bricks are numbered device by device, 2 a device, the one at local coarse position (cx, cy, cz) as (cx * 1 + cy) * 2 + cz.
All inputs are finite; a program needn't handle non-finite values.
Results may differ from the reference program's by a relative error of at most 0.015.
Values may be sent and summed in bfloat16 or wider, within the bound.
No kernel may reach another device: no remote copies, remote signals or barrier semaphores. Data moves between devices by JAX's collectives and lax.ppermute only.
A program may use at most 128 MiB of HBM per device.

```python
import math
import jax
import jax.numpy as jnp
from jax import lax

FCH = 32
CCH = 64
RX = 2
RY = 2
K = 2
RZ = 4
BF = 8
BC = 2
NBF = 1024
NBC = 256
LATX = 32
LATY = 16
N_GY = 8


def geometry(key):
    fill_key, order_key = jax.random.split(key)
    pos_x = jnp.arange(LATX, dtype=jnp.int32)[:, None, None]
    pos_y = jnp.arange(LATY, dtype=jnp.int32)[None, :, None]
    slot_rank = jnp.arange(K, dtype=jnp.int32)[None, None, :]
    depth_rank = jnp.arange(RZ, dtype=jnp.int32)[None, None, :]
    fill_count = jax.random.randint(fill_key, (LATX, LATY, 1), 1, K + 1)
    last_device = (pos_x >= LATX - RX) & (pos_y >= LATY - RY)
    fill_count = jnp.where(last_device, K, fill_count)
    first_column = (pos_x == 0) & (pos_y == 0)
    fill_count = jnp.where(first_column, 1, fill_count)
    scores = jax.random.randint(order_key, (LATX, LATY, RZ), 0, 1 << 20) * RZ + depth_rank
    top_corner = (pos_x == LATX - 1) & (pos_y == LATY - 1) & (depth_rank == RZ - 1)
    scores = jnp.where(top_corner, -1, scores)
    ranking = jnp.argsort(scores, axis=2)[:, :, :K].astype(jnp.int32)
    depths = jnp.sort(jnp.where(slot_rank < fill_count, ranking, RZ + slot_rank), axis=2)
    is_live = depths < RZ
    device = pos_x // RX * (LATY // RY) + pos_y // RY
    slot_ident = device * BF + (pos_x % RX * RY + pos_y % RY) * K + slot_rank
    full_x = jnp.broadcast_to(pos_x, depths.shape)
    full_y = jnp.broadcast_to(pos_y, depths.shape)
    lattice = jnp.full((LATX, LATY, RZ + 1), -1, jnp.int32)
    lattice = lattice.at[full_x, full_y, jnp.where(is_live, depths, RZ)].set(jnp.broadcast_to(slot_ident, depths.shape))
    entries = []
    for direction in range(27):
        step_x = direction // 9 - 1
        step_y = direction // 3 % 3 - 1
        step_z = direction % 3 - 1
        near_x = full_x + step_x
        near_y = full_y + step_y
        near_z = depths + step_z
        inside = (near_x >= 0) & (near_x < LATX) & (near_y >= 0) & (near_y < LATY) & (near_z >= 0) & (near_z < RZ) & is_live
        looked_up = lattice[jnp.clip(near_x, 0, LATX - 1), jnp.clip(near_y, 0, LATY - 1), jnp.clip(near_z, 0, RZ - 1)]
        entries.append(jnp.where(inside, looked_up, -1))
    adjacency_lat = jnp.stack(entries, axis=-1).astype(jnp.int32)
    coarse_local = (full_x % RX // 2 * (RY // 2) + full_y % RY // 2) * K + depths // 2
    octant = (full_x % 2 * 2 + full_y % 2) * 2 + depths % 2
    per_device = RX // 2 * (RY // 2) * K
    parent = jnp.where(is_live, (device * per_device + coarse_local) * 8 + octant, -1).astype(jnp.int32)
    return (adjacency_lat, parent)


def ordered(values):
    trailing = values.shape[3:]
    grouped = values.reshape((LATX // RX, RX, LATY // RY, RY, K) + trailing)
    reordered = jnp.moveaxis(grouped, 2, 1)
    return reordered.reshape((-1,) + trailing)


def draw_adjacency(key, part):
    adjacency_lat, parent = geometry(key)
    return ordered(adjacency_lat)


def draw_parents(key, part):
    adjacency_lat, parent = geometry(key)
    return ordered(parent)


def levels(stream_key, shape, shards, least, top_value):
    def one(position, blocks):
        steps = jax.random.uniform(jax.random.fold_in(jax.random.fold_in(stream_key, 6), position), (blocks,), jnp.float32, least / len(shards), top_value / len(shards))
        return jnp.repeat(jnp.exp(steps), shape[position] // blocks).reshape((-1,) + (1,) * (len(shape) - position - 1))

    loudness = one(*shards[0])
    for cut in shards[1:]:
        loudness = loudness * one(*cut)
    return loudness


def noise(key, extent, scale, reach, shards=(), kind=jnp.bfloat16):
    level = levels(key, extent, shards, -0.22, 0.18) if shards else 1.0
    values = jax.random.normal(key, extent, jnp.float32) * scale * level
    return jnp.minimum(jnp.maximum(values, -reach), reach).astype(kind)


def setup_inputs(seed: int = 0) -> dict:
    keys = jax.random.split(jax.random.key(seed), 8)
    return {
        "features": noise(keys[0], (NBF, FCH, 512), 1.0, 6.0, ((0, 128),)),
        "w_fine": noise(keys[1], (FCH, 27 * FCH), (27 * FCH) ** -0.5, 0.21875),
        "w_coarse": noise(keys[2], (CCH, 27 * FCH), (27 * FCH // 8) ** -0.5, 0.625),
        "w_up": noise(keys[3], (FCH, CCH), CCH ** -0.5, 0.75),
        "cotangent": noise(keys[4], (NBF, FCH, 512), 1.0, 6.0, ((0, 128),)),
        "adjacency": draw_adjacency(jax.random.fold_in(keys[7], 71), 0),
        "parents": draw_parents(jax.random.fold_in(keys[7], 71), 0),
    }


OFFSETS = [(outer_a - 1) * 100 + (outer_b - 1) * 10 + (outer_c - 1) for outer_a in range(3) for outer_b in range(3) for outer_c in range(3)]

def steps_of(direction):
    return (direction // 9 - 1, direction // 3 % 3 - 1, direction % 3 - 1)

def rim_slice(offset_step):
    if offset_step < 0:
        return slice(7, 8)
    if offset_step > 0:
        return slice(0, 1)
    return slice(0, 8)

def assemble(pieces):
    layers = []
    for along_x in range(3):
        strips = []
        for along_y in range(3):
            strips.append(jnp.concatenate([pieces[(along_x * 3 + along_y) * 3 + along_z] for along_z in range(3)], axis=4))
        layers.append(jnp.concatenate(strips, axis=3))
    padded = jnp.concatenate(layers, axis=2)
    return padded.reshape(padded.shape[0], padded.shape[1], 1000)

def brick_pieces(lookup, neighbours):
    pieces = []
    for direction in range(27):
        step_x, step_y, step_z = steps_of(direction)
        fetched = jnp.take(lookup, neighbours[:, direction], axis=0)
        voxels = fetched.reshape(fetched.shape[0], fetched.shape[1], 8, 8, 8)
        pieces.append(voxels[:, :, rim_slice(step_x), rim_slice(step_y), rim_slice(step_z)])
    return pieces

def stacked_taps(padded):
    return jnp.concatenate([padded[:, :, 111 + offset_now:889 + offset_now] for offset_now in OFFSETS], axis=1)

def interior(values):
    amount, channels = (values.shape[0], values.shape[1])
    padded = jnp.pad(values, ((0, 0), (0, 0), (111, 111)))
    return padded.reshape(amount, channels, 10, 10, 10)[:, :, 1:9, 1:9, 1:9].reshape(amount, channels, 512)

def into_range(values):
    amount, channels = (values.shape[0], values.shape[1])
    padded = jnp.pad(values.reshape(amount, channels, 8, 8, 8), ((0, 0), (0, 0), (1, 1), (1, 1), (1, 1)))
    return padded.reshape(amount, channels, 1000)[:, :, 111:889]

def flipped(weight, fan_channels):
    outputs = weight.shape[0]
    return jnp.transpose(weight.reshape(outputs, 27, fan_channels)[:, ::-1, :], (2, 1, 0)).reshape(fan_channels, 27 * outputs)

def to_brick(row_data):
    amount, channels = (row_data.shape[0] // 8, row_data.shape[1])
    blocks = row_data.reshape(amount, 2, 2, 2, channels, 4, 4, 4)
    return jnp.transpose(blocks, (0, 4, 1, 5, 2, 6, 3, 7)).reshape(amount, channels, 512)

def to_octants(bricks):
    amount, channels = (bricks.shape[0], bricks.shape[1])
    blocks = bricks.reshape(amount, channels, 2, 4, 2, 4, 2, 4)
    return jnp.transpose(blocks, (0, 2, 4, 6, 1, 3, 5, 7)).reshape(amount * 8, channels, 64)

def shrink(field_in):
    amount, channels = (field_in.shape[0], field_in.shape[1])
    return field_in.reshape(amount, channels, 4, 2, 4, 2, 4, 2).sum(axis=(3, 5, 7)).reshape(amount, channels, 64)

def enlarge(row_data):
    amount, channels = (row_data.shape[0], row_data.shape[1])
    voxels = row_data.reshape(amount, channels, 4, 1, 4, 1, 4, 1)
    return jnp.broadcast_to(voxels, (amount, channels, 4, 2, 4, 2, 4, 2)).reshape(amount, channels, 512)

def convolve_all(padded, weight, group_size):
    amount = padded.shape[0]
    grouped = padded.reshape(amount // group_size, group_size, padded.shape[1], 1000)

    def apply_one(bundle):
        tap_rows = stacked_taps(bundle).astype(jnp.float32)
        return interior(jnp.einsum('ok,bkq->boq', weight.astype(jnp.float32), tap_rows, precision=lax.Precision.HIGHEST))
    return lax.map(apply_one, grouped).reshape(amount, weight.shape[0], 512)

def weight_terms(padded, grad_in, group_size):
    amount = padded.shape[0]
    grouped = padded.reshape(amount // group_size, group_size, padded.shape[1], 1000)
    ranged = into_range(grad_in).reshape(amount // group_size, group_size, grad_in.shape[1], 778)

    def add_block(summed, operands):
        tap_rows = stacked_taps(operands[0]).astype(jnp.float32)
        return (summed + jnp.einsum('boq,bkq->ok', operands[1].astype(jnp.float32), tap_rows, precision=lax.Precision.HIGHEST), None)
    initial = jnp.zeros((grad_in.shape[1], 27 * padded.shape[1]), jnp.float32)
    summed, unused = lax.scan(add_block, initial, (grouped, ranged))
    return summed

def coarse_neighbours():
    half_x, half_y = (RX // 2, RY // 2)
    per_device = half_x * half_y * K
    coarse_ids = jnp.arange(NBC, dtype=jnp.int32)
    owner_dev = coarse_ids // per_device
    inside_id = coarse_ids % per_device
    lat_x = owner_dev // N_GY * half_x + inside_id // (half_y * K)
    lat_y = owner_dev % N_GY * half_y + inside_id // K % half_y
    lat_z = inside_id % K
    span_x = NBC // per_device // N_GY * half_x
    span_y = N_GY * half_y
    entries = []
    for direction in range(27):
        step_x, step_y, step_z = steps_of(direction)
        near_x = lat_x + step_x
        near_y = lat_y + step_y
        near_z = lat_z + step_z
        inside = (near_x >= 0) & (near_x < span_x) & (near_y >= 0) & (near_y < span_y) & (near_z >= 0) & (near_z < K)
        near_x = jnp.clip(near_x, 0, span_x - 1)
        near_y = jnp.clip(near_y, 0, span_y - 1)
        near_z = jnp.clip(near_z, 0, K - 1)
        target = (near_x // half_x * N_GY + near_y // half_y) * per_device + (near_x % half_x * half_y + near_y % half_y) * K + near_z
        entries.append(jnp.where(inside, target, NBC).astype(jnp.int32))
    return jnp.stack(entries, axis=1)

def with_zero(field_in):
    return jnp.concatenate([field_in, jnp.zeros((1,) + field_in.shape[1:], field_in.dtype)], axis=0)

def reference(features, w_fine, w_coarse, w_up, cotangent, adjacency, parents):
    fine_width = w_fine.shape[0]
    alive_mask = (adjacency[:, 13] >= 0).astype(jnp.float32)[:, None, None]
    fine_near = jnp.where(adjacency >= 0, adjacency, NBF).astype(jnp.int32)
    padded_x = assemble(brick_pieces(with_zero(features), fine_near))
    fine_out = (convolve_all(padded_x, w_fine, BF) * alive_mask).astype(jnp.bfloat16)
    slot_keys = jnp.where(parents >= 0, parents, NBC * 8).astype(jnp.int32)
    pooled_child = (shrink(fine_out.astype(jnp.float32)) * 0.125).astype(jnp.bfloat16)
    pooled_rows = jnp.zeros((NBC * 8 + 1, fine_width, 64), jnp.bfloat16).at[slot_keys].set(pooled_child)
    pooled = to_brick(pooled_rows[:NBC * 8])
    coarse_near = coarse_neighbours()
    padded_p = assemble(brick_pieces(with_zero(pooled), coarse_near))
    coarse_pre = convolve_all(padded_p, w_coarse, BC)
    coarse_act = jax.nn.silu(coarse_pre).astype(jnp.bfloat16)
    coarse_up = jnp.einsum('oi,biv->bov', w_up.astype(jnp.float32), coarse_act.astype(jnp.float32), precision=lax.Precision.HIGHEST)
    children = jnp.maximum(parents, 0).astype(jnp.int32)
    lifted = enlarge(jnp.take(to_octants(coarse_up), children, axis=0))
    layer_out = ((fine_out.astype(jnp.float32) + lifted) * alive_mask).astype(jnp.bfloat16)
    seed_grad = cotangent * alive_mask.astype(jnp.bfloat16)
    grad_rows = jnp.zeros((NBC * 8 + 1, fine_width, 64), jnp.float32).at[slot_keys].set(shrink(seed_grad.astype(jnp.float32)))
    grad_sum = to_brick(grad_rows[:NBC * 8])
    coarse_scale = 1.0 / math.sqrt(NBC * 512)
    grad_up = jnp.einsum('bov,biv->oi', grad_sum, coarse_act.astype(jnp.float32), precision=lax.Precision.HIGHEST) * coarse_scale
    back_up = jnp.einsum('oi,bov->biv', w_up.astype(jnp.float32), grad_sum, precision=lax.Precision.HIGHEST)
    sigmoid_v = jax.nn.sigmoid(coarse_pre)
    coarse_grad = (back_up * sigmoid_v * (1.0 + coarse_pre * (1.0 - sigmoid_v))).astype(jnp.bfloat16)
    grad_coarse = weight_terms(padded_p, coarse_grad, BC) * coarse_scale
    padded_g = assemble(brick_pieces(with_zero(coarse_grad), coarse_near))
    pooled_grad = convolve_all(padded_g, flipped(w_coarse, fine_width), BC)
    spread = enlarge(jnp.take(to_octants(pooled_grad), children, axis=0))
    fine_grad = ((seed_grad.astype(jnp.float32) + spread * 0.125) * alive_mask).astype(jnp.bfloat16)
    grad_fine = weight_terms(padded_x, fine_grad, BF) * (1.0 / math.sqrt(NBF * 512))
    padded_d = assemble(brick_pieces(with_zero(fine_grad), fine_near))
    grad_features = (convolve_all(padded_d, flipped(w_fine, fine_width), BF) * alive_mask).astype(jnp.bfloat16)
    return (layer_out, grad_features, grad_fine, grad_coarse, grad_up)
```

```python
import math

import jax
import jax.numpy as jnp
from jax import lax
from jax.experimental import pallas as pl
from jax.experimental.pallas import tpu as pltpu
from jax.sharding import PartitionSpec as P

BF = jnp.bfloat16
F32 = jnp.float32
AXES = ("gx", "gy")
NN = (((1,), (0,)), ((), ()))
NT = (((1,), (1,)), ((), ()))
TN = (((0,), (0,)), ((), ()))


def mm(a, b, dims=NN):
    return lax.dot_general(a, b, dims, preferred_element_type=F32)


def halves(value):
    even, odd = value[:, 0:8], value[:, 8:16]
    blank = jnp.zeros((value.shape[0], 1, value.shape[2]), value.dtype)
    odd_before = jnp.concatenate([blank, odd[:, 0:7]], axis=1)
    even_after = jnp.concatenate([even[:, 1:8], blank], axis=1)
    return even, odd, odd_before, even_after


def coarse_window(value):
    even, odd, odd_before, even_after = halves(value)
    blank = jnp.zeros_like(even)
    top = jnp.concatenate([odd_before, even, odd, blank], axis=2)
    low = jnp.concatenate([even, odd, even_after, blank], axis=2)
    return jnp.concatenate([top, low], axis=1)


def fine_window(value):
    even, odd, odd_before, even_after = halves(value)
    top = jnp.concatenate([odd_before[:, :, 32:64], even, odd[:, :, 0:32]], axis=2)
    low = jnp.concatenate([even[:, :, 32:64], odd, even_after[:, :, 0:32]], axis=2)
    return jnp.concatenate([top, low], axis=1)


def conv(ref, x_first, planes, y_first, width, weight):
    lanes = ref.shape[3]
    rows = planes * (width + 2) * 16
    stacked = jnp.concatenate(
        [
            ref[pl.ds(x_first + tap, planes), y_first : y_first + width + 2].reshape(rows, lanes)
            for tap in range(3)
        ],
        axis=1,
    )
    wide = mm(stacked, weight[...]).reshape(planes, width + 2, 16, 192)
    return (
        wide[:, 0:width, :, 0:64]
        + wide[:, 1 : width + 1, :, 64:128]
        + wide[:, 2 : width + 2, :, 128:192]
    )


def level_pair(
    feat, cot, meta, xm, xp, ym, yp, tf, tb, tc, tg, wu, wb,
    out, gfeat, sums,
    fw, cd, al, fo, pw, cg, act, gs, up, gw, yo,
):
    lane = lax.broadcasted_iota(jnp.int32, (128, 256), 1)
    row = lax.broadcasted_iota(jnp.int32, (128, 256), 0)
    same = (row >> 3) == ((lane & 127) >> 3)
    start = (row & 7) * 4 - 1
    depth_in = lane & 7
    res = lax.broadcasted_iota(jnp.int32, (32, 256), 1) & 3
    row_pair = lax.broadcasted_iota(jnp.int32, (16, 128), 0)
    row_pair = (row_pair & 7) * 2 + (row_pair >> 3)

    def place(code):
        return jnp.where(code > 0, code.astype(jnp.int32) * 8 - 8, -100)

    def source(cx, cy, k):
        if cy in (1, 2):
            if cx in (1, 2):
                slot = ((cx - 1) * 2 + cy - 1) * 2 + k
                return feat, cot, slot * 32, slot * 32, meta, slot
            ref = xm if cx == 0 else xp
            slot = (cy - 1) * 2 + k
            sender = ((1 if cx == 0 else 0) * 2 + cy - 1) * 2 + k
            return ref, ref, slot * 32, 128 + slot * 32, ref, 256 + sender
        ref = ym if cy == 0 else yp
        slot = cx * 2 + k
        block = (0, 1, 1, 2)[cx]
        side = (1, 0, 1, 0)[cx]
        sender = (side * 2 + (1 if cy == 0 else 0)) * 2 + k
        return ref, ref, slot * 32, 256 + slot * 32, ref, 512 + block * 16 + sender

    def codes(cx, cy):
        rows = []
        for k in range(2):
            ref, index = source(cx, cy, k)[4:]
            base = index // 16 * 16
            rows.append(ref[base : base + 16, 0:128].astype(F32)[index - base : index - base + 1])
        return rows

    for cx in range(4):
        for cy in range(4):
            code = codes(cx, cy)
            begin = jnp.concatenate([place(value) for value in code], axis=1)
            shift = begin + depth_in - start
            pick_even = (same & (shift >= 0) & (shift < 4)).astype(F32).astype(BF)
            pick_odd = (same & (shift >= 2) & (shift < 6)).astype(F32).astype(BF)
            live = jnp.zeros((16, 128), F32)
            for value in code:
                live = live + ((row_pair >> 2) == (value.astype(jnp.int32) - 1)).astype(F32)
            for y in range(8):
                al[cx, cy * 8 + y] = live
            fields = []
            for k in range(2):
                ref_f, ref_c, at_f, at_c = source(cx, cy, k)[:4]
                fields.append((ref_f, at_f, ref_c, at_c))
            for g in range(4):
                cut = slice(g * 128, g * 128 + 128)
                f = jnp.concatenate([r[a : a + 32, cut] for r, a, _, _ in fields], axis=1)
                c = jnp.concatenate([r[a : a + 32, cut] for _, _, r, a in fields], axis=1)
                none = jnp.zeros_like(f)
                fr = [jnp.where(res == i, f, none) for i in range(4)]
                cr = [jnp.where(res == i, c, none) for i in range(4)]
                even = jnp.concatenate([fr[3], fr[0], fr[1], fr[2], cr[0], cr[1]], axis=0)
                odd = jnp.concatenate([fr[1], fr[2], fr[3], fr[0], cr[2], cr[3]], axis=0)
                even = mm(pick_even, even, NT).reshape(16, 8, 192)
                odd = mm(pick_odd, odd, NT).reshape(16, 8, 192)
                both = jnp.concatenate([even, odd], axis=1)
                xs = slice(cx * 8 + 2 * g, cx * 8 + 2 * g + 2)
                ys = slice(cy * 8, cy * 8 + 8)
                fw[xs, ys] = both[:, :, 0:128].astype(BF).reshape(2, 8, 16, 128)
                cd[xs, ys] = both[:, :, 128:192].astype(BF).reshape(2, 8, 16, 64)

    def fine_step(step, carry):
        value = conv(fw, 1 + 2 * step, 2, 1, 28, tf)
        mask = al[(2 + 2 * step) // 8, 2:30, :, 0:64]
        fine = (value * mask[None]).astype(BF)
        fo[pl.ds(2 * step, 2)] = fine[:, 6:22]
        fine = fine.astype(F32)
        pooled = (fine[0] + fine[1]).reshape(14, 2, 16, 64)
        pooled = pooled[:, 0] + pooled[:, 1]
        pooled = (pooled[:, :, 0:32] + pooled[:, :, 32:64]) * 0.125
        pw[1 + step, 1:15] = coarse_window(pooled).astype(BF)
        return carry

    lax.fori_loop(0, 14, fine_step, 0)

    def coarse_step(step, carry):
        pre = conv(pw, 1 + step, 1, 1, 12, tc)[0]
        sig = 1.0 / (1.0 + jnp.exp(-pre))
        silu = (pre * sig).astype(BF)
        act[step] = silu
        up[step] = mm(silu.reshape(192, 64), wu[...]).reshape(12, 16, 64)
        pair = cd[pl.ds(4 + 2 * step, 2), 4:28].astype(F32)
        pair = (pair[0] + pair[1]).reshape(12, 2, 16, 64)
        pair = pair[:, 0] + pair[:, 1]
        high = pair.astype(BF)
        low = (pair - high.astype(F32)).astype(BF)
        split = jnp.concatenate([high, low], axis=2)
        gs[step] = split
        back = mm(split.reshape(192, 128), wb[...]).reshape(12, 16, 64)
        grad = back * sig * (1.0 + pre * (1.0 - sig))
        cg[step] = coarse_window(grad).astype(BF)
        return carry

    lax.fori_loop(0, 12, coarse_step, 0)

    def spread_step(step, carry):
        pooled_grad = conv(cg, step, 1, 0, 10, tg)[0] * 0.125
        spread = jnp.broadcast_to(pooled_grad[:, None], (10, 2, 16, 64)).reshape(20, 16, 64)
        for half in range(2):
            x = 6 + 2 * step + half
            seed = cd[x, 6:26].astype(F32)
            grad = (seed + spread) * al[x // 8, 6:26, :, 0:64]
            gw[2 * step + half] = fine_window(grad).astype(BF)
        return carry

    lax.fori_loop(0, 10, spread_step, 0)

    def back_step(step, carry):
        value = conv(gw, 1 + 2 * step, 2, 1, 16, tb)
        lifted = up[2 + step, 2:10]
        lifted = jnp.broadcast_to(lifted[:, None], (8, 2, 16, 64)).reshape(16, 16, 64)
        layer = fo[pl.ds(6 + 2 * step, 2)].astype(F32) + lifted[None]
        yo[pl.ds(2 * step, 2)] = jnp.concatenate([layer, value], axis=3).astype(BF)
        return carry

    lax.fori_loop(0, 8, back_step, 0)

    lane = lax.broadcasted_iota(jnp.int32, (256, 256), 1)
    row = lax.broadcasted_iota(jnp.int32, (256, 256), 0)
    same = (row >> 4) == ((lane & 127) >> 3)
    target = (row & 7) * 2 + ((row >> 3) & 1)
    even_lane = (lax.broadcasted_iota(jnp.int32, (32, 256), 1) & 1) == 0
    for cx in range(2):
        for cy in range(2):
            code = codes(cx + 1, cy + 1)
            begin = jnp.concatenate([place(value) for value in code], axis=1)
            pick = (same & (((begin + (lane & 7)) >> 1) == target)).astype(F32).astype(BF)
            first = (cx * 2 + cy) * 64
            for g in range(4):
                rows = yo[cx * 8 + 2 * g : cx * 8 + 2 * g + 2, cy * 8 : cy * 8 + 8]
                moved = mm(rows.reshape(256, 128), pick, TN)
                layer = jnp.where(even_lane, moved[0:32], moved[32:64]).astype(BF)
                grad = jnp.where(even_lane, moved[64:96], moved[96:128]).astype(BF)
                cut = slice(g * 128, g * 128 + 128)
                out[first : first + 32, cut] = layer[:, 0:128]
                out[first + 32 : first + 64, cut] = layer[:, 128:256]
                gfeat[first : first + 32, cut] = grad[:, 0:128]
                gfeat[first + 32 : first + 64, cut] = grad[:, 128:256]

    def fine_terms(step, total):
        grad = gw[pl.ds(2 + 2 * step, 2), 2:18].reshape(512, 128)[:, 32:96]
        taps = [
            fw[pl.ds(7 + 2 * step + tap // 3, 2), 7 + tap % 3 : 23 + tap % 3].reshape(512, 128)
            for tap in range(9)
        ]
        return total + mm(grad, jnp.concatenate(taps, axis=1), TN)

    total = lax.fori_loop(0, 8, fine_terms, jnp.zeros((64, 1152), F32))
    fine_scale = 1.0 / math.sqrt(524288)
    coarse_scale = 1.0 / math.sqrt(131072)
    sums[...] = jnp.zeros_like(sums)
    for tap in range(9):
        at = tap * 128
        term = total[0:32, at : at + 96] + total[32:64, at + 32 : at + 128]
        sums[0:32, tap * 96 : tap * 96 + 96] = term * fine_scale

    def coarse_terms(step, totals):
        total, total_up = totals
        grad = cg[pl.ds(2 + 4 * step, 4), 2:10].reshape(512, 256)[:, 64:128]
        taps = [
            pw[pl.ds(3 + 4 * step + tap // 3, 4), 3 + tap % 3 : 11 + tap % 3].reshape(512, 128)
            for tap in range(9)
        ]
        total = total + mm(grad, jnp.concatenate(taps, axis=1), TN)
        silu = act[pl.ds(2 + 4 * step, 4), 2:10].reshape(512, 64)
        split = gs[pl.ds(2 + 4 * step, 4), 2:10].reshape(512, 128)
        return total, total_up + mm(silu, split, TN)

    total, total_up = lax.fori_loop(
        0, 2, coarse_terms, (jnp.zeros((64, 1152), F32), jnp.zeros((64, 128), F32))
    )
    for tap in range(9):
        at = tap * 128
        sums[32:96, tap * 96 : tap * 96 + 96] = total[:, at : at + 96] * coarse_scale
    total_up = total_up[:, 0:32] + total_up[:, 32:64] + total_up[:, 64:96] + total_up[:, 96:128]
    sums[32:96, 864:896] = total_up * coarse_scale


def tap_table(weight, lanes):
    parts = jnp.transpose(weight.reshape(32, 3, 3, 3, 32), (1, 3, 4, 2, 0))
    first = jnp.pad(parts, ((0, 0), (0, 1), (0, 0), (0, 0), (0, 0)))
    second = jnp.pad(parts, ((0, 0), (1, 0), (0, 0), (0, 0), (0, 0)))
    return jnp.stack([first, second], axis=4).reshape(384, 192)


def step_pairs(dx, dy, wide, across):
    pairs = []
    for x in range(wide):
        for y in range(across):
            if 0 <= x + dx < wide and 0 <= y + dy < across:
                pairs.append((x * across + y, (x + dx) * across + y + dy))
    return pairs


def local(features, w_fine, w_coarse, w_up, cotangent, adjacency, parents):
    wide, across = lax.axis_size("gx"), lax.axis_size("gy")
    feat = features.reshape(256, 512)
    cot = cotangent.reshape(256, 512)
    depth = ((parents >> 3) & 1) * 2 + (parents & 1)
    code = jnp.where(parents >= 0, depth + 1, 0).astype(BF)
    meta = jnp.broadcast_to(jnp.pad(code, (0, 8))[:, None], (16, 512))
    send_up = jnp.concatenate([feat[128:256], cot[128:256], meta])
    send_down = jnp.concatenate([feat[0:128], cot[0:128], meta])
    xm = lax.ppermute(send_up, AXES, step_pairs(1, 0, wide, across))
    xp = lax.ppermute(send_down, AXES, step_pairs(-1, 0, wide, across))

    def edge(y):
        at = y * 64
        parts = []
        for base, own in ((0, feat), (128, cot)):
            parts.append(xm[base + at : base + at + 64])
            parts.append(own[at : at + 64])
            parts.append(own[128 + at : 128 + at + 64])
            parts.append(xp[base + at : base + at + 64])
        return jnp.concatenate(parts + [xm[256:272], meta, xp[256:272]])

    ym = lax.ppermute(edge(1), AXES, step_pairs(0, 1, wide, across))
    yp = lax.ppermute(edge(0), AXES, step_pairs(0, -1, wide, across))

    tf = tap_table(w_fine, 128)
    flipped = jnp.transpose(w_fine.reshape(32, 27, 32)[:, ::-1], (2, 1, 0))
    tb = tap_table(flipped, 128)
    parts = w_coarse.reshape(64, 3, 3, 96)
    tc = jnp.pad(jnp.transpose(parts, (1, 3, 2, 0)), ((0, 0), (0, 32), (0, 0), (0, 0)))
    tc = tc.reshape(384, 192)
    parts = w_coarse.reshape(64, 3, 3, 3, 32)[:, ::-1, ::-1, ::-1]
    tg = jnp.transpose(parts, (1, 3, 0, 2, 4)).reshape(3, 192, 3, 1, 32)
    tg = jnp.pad(jnp.broadcast_to(tg, (3, 192, 3, 2, 32)).reshape(3, 192, 192), ((0, 0), (0, 64), (0, 0)))
    tg = tg.reshape(768, 192)
    wu = jnp.concatenate([w_up, w_up]).T
    wb = jnp.concatenate([w_up] * 4)

    out, gfeat, sums = pl.pallas_call(
        level_pair,
        out_shape=(
            jax.ShapeDtypeStruct((256, 512), BF),
            jax.ShapeDtypeStruct((256, 512), BF),
            jax.ShapeDtypeStruct((96, 896), F32),
        ),
        in_specs=[pl.BlockSpec(memory_space=pltpu.VMEM)] * 13,
        out_specs=(pl.BlockSpec(memory_space=pltpu.VMEM),) * 3,
        scratch_shapes=[
            pltpu.VMEM((32, 32, 16, 128), BF),
            pltpu.VMEM((32, 32, 16, 64), BF),
            pltpu.VMEM((4, 32, 16, 128), F32),
            pltpu.VMEM((28, 16, 16, 64), BF),
            pltpu.VMEM((16, 16, 16, 128), BF),
            pltpu.VMEM((12, 12, 16, 256), BF),
            pltpu.VMEM((12, 12, 16, 64), BF),
            pltpu.VMEM((12, 12, 16, 128), BF),
            pltpu.VMEM((12, 12, 16, 64), F32),
            pltpu.VMEM((20, 20, 16, 128), BF),
            pltpu.VMEM((16, 16, 16, 128), BF),
        ],
        compiler_params=pltpu.CompilerParams(vmem_limit_bytes=50 * 1024 * 1024),
    )(feat, cot, meta, xm, xp, ym, yp, tf, tb, tc, tg, wu, wb)

    share = sums.reshape(16, 42, 128).astype(BF)
    share = lax.all_to_all(share, "gx", 0, 0, tiled=True).astype(F32).sum(0)
    for bit in range(3):
        pairs = [(i, i ^ (1 << bit)) for i in range(across)]
        other = lax.ppermute(share.astype(BF), "gy", pairs)
        share = share.astype(BF).astype(F32) + other.astype(F32)
    shares = jnp.broadcast_to(share.astype(BF)[None], (16, 42, 128))
    total = lax.all_to_all(shares, "gx", 0, 0, tiled=True).reshape(96, 896).astype(F32)
    return (
        out.reshape(features.shape),
        gfeat.reshape(features.shape),
        total[0:32, 0:864],
        total[32:96, 0:864],
        total[32:96, 864:896].T,
    )


def solution(mesh):
    return jax.shard_map(
        local,
        mesh=mesh,
        in_specs=(
            P(("gx", "gy"), None, None),
            P(),
            P(),
            P(),
            P(("gx", "gy"), None, None),
            P(("gx", "gy"), None),
            P(("gx", "gy")),
        ),
        out_specs=(P(("gx", "gy"), None, None), P(("gx", "gy"), None, None), P(), P(), P()),
        check_vma=False,
    )
```

```python
import functools
import math

import jax
import jax.numpy as jnp
from jax import lax
from jax.experimental import pallas as pl
from jax.experimental.pallas import tpu as pltpu
from jax.sharding import PartitionSpec as P

BF = jnp.bfloat16
F32 = jnp.float32
AXES = ("gx", "gy")
NN = (((1,), (0,)), ((), ()))
NT = (((1,), (1,)), ((), ()))
TN = (((0,), (0,)), ((), ()))


def mm(a, b, dims=NN):
    return lax.dot_general(a, b, dims, preferred_element_type=F32)


def halves(value):
    even, odd = value[:, 0:8], value[:, 8:16]
    blank = jnp.zeros((value.shape[0], 1, value.shape[2]), value.dtype)
    odd_before = jnp.concatenate([blank, odd[:, 0:7]], axis=1)
    even_after = jnp.concatenate([even[:, 1:8], blank], axis=1)
    return even, odd, odd_before, even_after


def coarse_window(value):
    even, odd, odd_before, even_after = halves(value)
    blank = jnp.zeros_like(even)
    top = jnp.concatenate([odd_before, even, odd, blank], axis=2)
    low = jnp.concatenate([even, odd, even_after, blank], axis=2)
    return jnp.concatenate([top, low], axis=1)


def fine_window(value):
    even, odd, odd_before, even_after = halves(value)
    top = jnp.concatenate([odd_before[:, :, 32:64], even, odd[:, :, 0:32]], axis=2)
    low = jnp.concatenate([even[:, :, 32:64], odd, even_after[:, :, 0:32]], axis=2)
    return jnp.concatenate([top, low], axis=1)


def place(code):
    return jnp.where(code > 0, code.astype(jnp.int32) * 8 - 8, -100)


def meta_row(ref, base, slot):
    return ref[base : base + 16, 0:128].astype(F32)[slot : slot + 1]


def roll(value, by):
    return pltpu.roll(value.astype(F32), by, 1).astype(BF)


def source(cx, cy, refs):
    if cy in (1, 2) and cx in (1, 2):
        feat, cot, meta = refs
        first = ((cx - 1) * 2 + cy - 1) * 2

        def cut(ref, k, g):
            at = (first + k) * 32
            return ref[at : at + 32, g * 128 : g * 128 + 128]

        return (
            lambda k, g: cut(feat, k, g),
            lambda k, g: cut(cot, k, g),
            [meta_row(meta, 0, first + k) for k in range(2)],
        )
    (ref,) = refs
    if cy in (1, 2):
        first = (cy - 1) * 2
        sender = ((1 if cx == 0 else 0) * 2 + cy - 1) * 2

        def features(k, g):
            at = ((first + k) * 4 + g) * 32
            return ref[at : at + 32]

        def cotangents(k, g):
            at = 512 + ((first + k) * 2 + g % 2) * 32
            return ref[at : at + 32]

        return features, cotangents, [meta_row(ref, 768, sender + k) for k in range(2)]
    sender = ((1, 0, 1, 0)[cx] * 2 + (1 if cy == 0 else 0)) * 2
    base = 1408 + (0, 1, 1, 2)[cx] * 16

    def features(k, g):
        at = ((cx * 2 + k) * 4 + g) * 32
        return ref[at : at + 32]

    def cotangents(k, g):
        at = 1024 + ((max(cx * 2 - 1, 0) + (g // 2 if cx in (1, 2) else 0)) * 2 + k) * 32
        packed = ref[at : at + 32]
        return packed if g % 2 == 0 else roll(packed, 32 if cy == 0 else 96)

    return features, cotangents, [meta_row(ref, base, sender + k) for k in range(2)]


def live_rows(code):
    pair = lax.broadcasted_iota(jnp.int32, (16, 128), 0)
    pair = (pair & 7) * 2 + (pair >> 3)
    live = jnp.zeros((16, 128), F32)
    for value in code:
        live = live + ((pair >> 2) == (value.astype(jnp.int32) - 1)).astype(F32)
    return live


def place_column(cx, cy, refs, fw, cd, x_at, y_at):
    features, cotangents, code = source(cx, cy, refs)
    lane = lax.broadcasted_iota(jnp.int32, (128, 256), 1)
    row = lax.broadcasted_iota(jnp.int32, (128, 256), 0)
    same = (row >> 3) == ((lane & 127) >> 3)
    res = lax.broadcasted_iota(jnp.int32, (32, 256), 1) & 3
    begin = jnp.concatenate([place(value) for value in code], axis=1)
    shift = begin + (lane & 7) - ((row & 7) * 4 - 1)
    pick_even = (same & (shift >= 0) & (shift < 4)).astype(F32).astype(BF)
    pick_odd = (same & (shift >= 2) & (shift < 6)).astype(F32).astype(BF)
    wanted = {0: (2, 3), 1: (0, 1, 2, 3), 2: (0, 1, 2, 3), 3: (0, 1)}[cx]
    for g in range(4):
        f = jnp.concatenate([features(k, g) for k in range(2)], axis=1)
        none = jnp.zeros_like(f)
        fr = [jnp.where(res == i, f, none) for i in range(4)]
        even, odd = [fr[3], fr[0], fr[1], fr[2]], [fr[1], fr[2], fr[3], fr[0]]
        if g in wanted:
            c = jnp.concatenate([cotangents(k, g) for k in range(2)], axis=1)
            cr = [jnp.where(res == i, c, none) for i in range(4)]
            even, odd = even + cr[0:2], odd + cr[2:4]
        lanes = 32 * len(even)
        even = mm(pick_even, jnp.concatenate(even, axis=0), NT).reshape(16, 8, lanes)
        odd = mm(pick_odd, jnp.concatenate(odd, axis=0), NT).reshape(16, 8, lanes)
        both = jnp.concatenate([even, odd], axis=1)
        xs = slice(x_at + 2 * g, x_at + 2 * g + 2)
        ys = slice(y_at, y_at + 8)
        fw[xs, ys] = both[:, :, 0:128].astype(BF).reshape(2, 8, 16, 128)
        if g in wanted:
            cd[xs, ys] = both[:, :, 128:192].astype(BF).reshape(2, 8, 16, 64)
    return code


def pack_x(
    parents_far, feat_far, cot_far, up, down, meta, feat, cot, parents, sems,
):
    copies = [
        pltpu.make_async_copy(far, near, sems.at[i])
        for i, (far, near) in enumerate(
            (
                (parents_far, parents),
                (feat_far, feat),
                (cot_far, cot),
            )
        )
    ]
    for copy in copies:
        copy.start()
    for copy in copies:
        copy.wait()
    row = lax.broadcasted_iota(jnp.int32, (16, 128), 0)
    code = jnp.zeros((16, 128), F32)
    for slot in range(8):
        value = parents[slot]
        depth = jnp.where(value >= 0, ((value >> 3) & 1) * 2 + (value & 1) + 1, 0)
        code = jnp.where(row == slot, depth.astype(F32), code)
    code = code.astype(BF)
    meta[...] = code
    for ref, side in ((up, 1), (down, 0)):
        for slot in range(4):
            at = (side * 4 + slot) * 32
            for g in range(4):
                to = (slot * 4 + g) * 32
                ref[to : to + 32] = feat[at : at + 32, g * 128 : g * 128 + 128]
            for part in range(2):
                to = 512 + (slot * 2 + part) * 32
                lanes = slice((2 * side + part) * 128, (2 * side + part) * 128 + 128)
                ref[to : to + 32] = cot[at : at + 32, lanes]
        ref[768:784] = code


def pack_y(feat, cot, meta, xm, xp, up, down):
    high = (lax.broadcasted_iota(jnp.int32, (32, 128), 1) & 32) != 0
    for ref, side in ((up, 1), (down, 0)):
        pair = 0
        for cx in range(4):
            features, cotangents, _ = source(
                cx, side + 1, (xm,) if cx == 0 else (xp,) if cx == 3 else (feat, cot, meta)
            )
            for k in range(2):
                for g in range(4):
                    to = ((cx * 2 + k) * 4 + g) * 32
                    ref[to : to + 32] = features(k, g)
            for g in {0: (2,), 1: (0, 2), 2: (0, 2), 3: (0,)}[cx]:
                for k in range(2):
                    to = 1024 + (pair * 2 + k) * 32
                    first, second = cotangents(k, g), cotangents(k, g + 1)
                    if side == 1:
                        ref[to : to + 32] = jnp.where(high, first, roll(second, 96))
                    else:
                        ref[to : to + 32] = jnp.where(high, roll(second, 32), first)
                pair += 1
        ref[1408:1424] = xm[768:784]
        ref[1424:1440] = meta[...]
        ref[1440:1456] = xp[768:784]


def prepare(
    feat, cot, meta, w_fine, w_coarse,
    fw, cd, tf, tb, tc, tg, fo, pw,
    turned_f, turned_c, al,
):
    turned_f[...] = jnp.zeros_like(turned_f)
    turned_c[...] = jnp.zeros_like(turned_c)
    tb[...] = jnp.zeros_like(tb)
    tg[...] = jnp.zeros_like(tg)
    for tx in range(3):
        for ty in range(3):
            at = (tx * 3 + ty) * 96
            for zo in range(2):
                to, lanes = (ty * 2 + zo) * 32, tx * 128 + zo * 32
                turned_f[to : to + 32, lanes : lanes + 96] = w_fine[:, at : at + 96].astype(F32)
            turned_c[ty * 64 : ty * 64 + 64, tx * 128 : tx * 128 + 96] = w_coarse[
                :, at : at + 96
            ].astype(F32)
            for tz in range(3):
                at = (((2 - tx) * 3 + 2 - ty) * 3 + 2 - tz) * 32
                for zo in range(2):
                    lanes = (ty * 2 + zo) * 32
                    to = tx * 128 + (tz + zo) * 32
                    tb[to : to + 32, lanes : lanes + 32] = w_fine[:, at : at + 32]
                    to = tx * 256 + tz * 64
                    tg[to : to + 64, lanes : lanes + 32] = w_coarse[:, at : at + 32]
    row = lax.broadcasted_iota(jnp.int32, (384, 384), 0)
    eye = (row == lax.broadcasted_iota(jnp.int32, (384, 384), 1)).astype(F32).astype(BF)
    tf[...] = mm(eye, turned_f[...].astype(BF), NT).astype(BF)
    tc[...] = mm(eye, turned_c[...].astype(BF), NT).astype(BF)
    for cx in (1, 2):
        for cy in (1, 2):
            refs = (feat, cot, meta)
            code = place_column(cx, cy, refs, fw, cd, cx * 8 - 8, cy * 8 - 8)
            live = live_rows(code)
            for y in range(8):
                al[cx - 1, cy * 8 - 8 + y] = live
    for at in range(6):
        value = conv(fw, 1 + 2 * at, 2, 1, 12, tf)
        fine = (value * al[(2 + 2 * at) // 8, 2:14, :, 0:64][None]).astype(BF)
        pw[at] = pool(fine)
        fo[2 * at : 2 * at + 2] = fine


def conv_rows(ref, x_first, planes, y_first, width):
    rows = planes * (width + 2) * 16
    return jnp.concatenate(
        [
            ref[pl.ds(x_first + tap, planes), y_first : y_first + width + 2].reshape(
                rows, ref.shape[3]
            )
            for tap in range(3)
        ],
        axis=1,
    )


def conv_taps(wide, width):
    return (
        wide[:, 0:width, :, 0:64]
        + wide[:, 1 : width + 1, :, 64:128]
        + wide[:, 2 : width + 2, :, 128:192]
    )


def conv(ref, x_first, planes, y_first, width, weight):
    rows = conv_rows(ref, x_first, planes, y_first, width)
    return conv_taps(mm(rows, weight[...]).reshape(planes, width + 2, 16, 192), width)


def pool(fine):
    rows = fine.shape[1] // 2
    pooled = fine.astype(F32)
    pooled = (pooled[0] + pooled[1]).reshape(rows, 2, 16, 64)
    pooled = pooled[:, 0] + pooled[:, 1]
    return coarse_window((pooled[:, :, 0:32] + pooled[:, :, 32:64]) * 0.125).astype(BF)


def middle(xm, xp, meta, own_fw, own_cd, tf, fw, cd, fo, pw, al):
    fw[8:24] = own_fw[...]
    cd[8:24] = own_cd[...]
    for cx in range(4):
        for cy in (1, 2):
            if cx in (0, 3):
                refs = (xm,) if cx == 0 else (xp,)
                code = place_column(cx, cy, refs, fw, cd, cx * 8, cy * 8 - 8)
            else:
                code = [meta_row(meta, 0, ((cx - 1) * 2 + cy - 1) * 2 + k) for k in range(2)]
            live = live_rows(code)
            for y in range(8):
                al[cx, cy * 8 - 8 + y] = live

    for order, at in enumerate((0, 1, 2, 3, 10, 11, 12, 13)):
        value = conv(fw, 1 + 2 * at, 2, 1, 12, tf)
        fine = (value * al[(2 + 2 * at) // 8, 2:14, :, 0:64][None]).astype(BF)
        pw[order] = pool(fine)
        fo[2 * order : 2 * order + 2] = fine


def main(
    xm, xp, ym, yp, meta, mid_fw, mid_cd, mid_fo, mid_pw, in_fo, in_pw, tf, tc, tg, w_up,
    gw, fo, up, keep, send,
    fw, cd, al, pw, cg, act, gs, sums,
):
    fw[:, 8:24] = mid_fw[...]
    cd[:, 8:24] = mid_cd[...]
    fo[0:8, 2:14] = mid_fo[0:8]
    fo[8:20, 2:14] = in_fo[...]
    fo[20:28, 2:14] = mid_fo[8:16]
    pw[1:5, 5:11] = mid_pw[0:4]
    pw[5:11, 5:11] = in_pw[...]
    pw[11:15, 5:11] = mid_pw[4:8]
    for cx in range(4):
        for cy in range(4):
            if cy in (0, 3):
                refs = (ym,) if cy == 0 else (yp,)
                code = place_column(cx, cy, refs, fw, cd, cx * 8, cy * 8)
            else:
                refs = (xm,) if cx == 0 else (xp,) if cx == 3 else (meta, meta, meta)
                code = source(cx, cy, refs)[2]
            live = live_rows(code)
            for y in range(8):
                al[cx, cy * 8 + y] = live

    def fine_step(step, carry):
        rows = [conv_rows(fw, 1 + 2 * step, 2, first, 8) for first in (1, 21)]
        wide = mm(jnp.concatenate(rows, axis=0), tf[...]).reshape(2, 2, 10, 16, 192)
        column = (2 + 2 * step) // 8
        first = (conv_taps(wide[0], 8) * al[column, 2:10, :, 0:64][None]).astype(BF)
        second = (conv_taps(wide[1], 8) * al[column, 22:30, :, 0:64][None]).astype(BF)
        pw[1 + step, 1:5] = pool(first)
        pw[1 + step, 11:15] = pool(second)

        fo[pl.ds(2 * step, 2), 0:2] = first[:, 6:8]
        fo[pl.ds(2 * step, 2), 14:16] = second[:, 0:2]
        return carry

    lax.fori_loop(0, 14, fine_step, 0, unroll=14)

    twice = jnp.concatenate([w_up[...]] * 2, axis=0)
    four = jnp.concatenate([w_up[...]] * 4, axis=0)

    def coarse_step(step, carry):
        pre = conv(pw, 1 + step, 1, 1, 12, tc)[0]
        sig = 1.0 / (1.0 + jnp.exp(-pre))
        silu = (pre * sig).astype(BF)
        act[step] = silu
        up[step] = mm(silu.reshape(192, 64), twice, NT).reshape(12, 16, 64)
        pair = cd[pl.ds(4 + 2 * step, 2), 4:28].astype(F32)
        pair = (pair[0] + pair[1]).reshape(12, 2, 16, 64)
        pair = pair[:, 0] + pair[:, 1]
        high = pair.astype(BF)
        low = (pair - high.astype(F32)).astype(BF)
        split = jnp.concatenate([high, low], axis=2)
        gs[step] = split
        back = mm(split.reshape(192, 128), four).reshape(12, 16, 64)
        grad = back * sig * (1.0 + pre * (1.0 - sig))
        cg[step] = coarse_window(grad).astype(BF)
        return carry

    lax.fori_loop(0, 12, coarse_step, 0, unroll=6)

    def spread_step(step, carry):
        pooled_grad = conv(cg, step, 1, 0, 10, tg)[0] * 0.125
        spread = jnp.broadcast_to(pooled_grad[:, None], (10, 2, 16, 64)).reshape(20, 16, 64)
        for half in range(2):
            x = 6 + 2 * step + half
            seed = cd[x, 6:26].astype(F32)
            grad = (seed + spread) * al[x // 8, 6:26, :, 0:64]
            gw[2 * step + half] = fine_window(grad).astype(BF)
        return carry

    lax.fori_loop(0, 10, spread_step, 0, unroll=5)

    def fine_terms(step, total):
        grad = gw[pl.ds(2 + 2 * step, 2), 2:18].reshape(512, 128)[:, 32:96]
        taps = [
            fw[pl.ds(7 + 2 * step + tap // 3, 2), 7 + tap % 3 : 23 + tap % 3].reshape(512, 128)
            for tap in range(9)
        ]
        return total + mm(grad, jnp.concatenate(taps, axis=1), TN)

    total = lax.fori_loop(0, 8, fine_terms, jnp.zeros((64, 1152), F32), unroll=8)
    fine_scale = 1.0 / math.sqrt(524288)
    coarse_scale = 1.0 / math.sqrt(131072)
    sums[...] = jnp.zeros_like(sums)
    for tap in range(9):
        at = tap * 128
        term = total[0:32, at : at + 96] + total[32:64, at + 32 : at + 128]
        sums[0:32, tap * 96 : tap * 96 + 96] = term * fine_scale

    def coarse_terms(step, totals):
        total, total_up = totals
        grad = cg[pl.ds(2 + 4 * step, 4), 2:10].reshape(512, 256)[:, 64:128]
        taps = [
            pw[pl.ds(3 + 4 * step + tap // 3, 4), 3 + tap % 3 : 11 + tap % 3].reshape(512, 128)
            for tap in range(9)
        ]
        total = total + mm(grad, jnp.concatenate(taps, axis=1), TN)
        silu = act[pl.ds(2 + 4 * step, 4), 2:10].reshape(512, 64)
        split = gs[pl.ds(2 + 4 * step, 4), 2:10].reshape(512, 128)
        return total, total_up + mm(split, silu, TN)

    total, total_up = lax.fori_loop(
        0, 2, coarse_terms, (jnp.zeros((64, 1152), F32), jnp.zeros((128, 64), F32)), unroll=2
    )
    for tap in range(9):
        at = tap * 128
        sums[32:96, tap * 96 : tap * 96 + 96] = total[:, at : at + 96] * coarse_scale
    total_up = total_up[0:32] + total_up[32:64] + total_up[64:96] + total_up[96:128]
    sums[0:32, 864:896] = total_up[:, 0:32] * coarse_scale
    sums[32:64, 864:896] = total_up[:, 32:64] * coarse_scale
    core = lax.axis_index("gy") % 2
    low, high = sums[0:48], sums[48:96]
    keep[...] = jnp.where(core == 0, low, high).astype(BF)
    send[...] = jnp.where(core == 0, high, low).astype(BF)


def to_bricks(meta, rows_of, ref):
    lane = lax.broadcasted_iota(jnp.int32, (256, 256), 1)
    row = lax.broadcasted_iota(jnp.int32, (256, 256), 0)
    same = (row >> 4) == ((lane & 127) >> 3)
    target = (row & 7) * 2 + ((row >> 3) & 1)
    even_lane = (lax.broadcasted_iota(jnp.int32, (32, 256), 1) & 1) == 0
    for cx in range(2):
        for cy in range(2):
            code = [meta_row(meta, 0, (cx * 2 + cy) * 2 + k) for k in range(2)]
            begin = jnp.concatenate([place(value) for value in code], axis=1)
            pick = (same & (((begin + (lane & 7)) >> 1) == target)).astype(F32).astype(BF)
            first = (cx * 2 + cy) * 64
            for g in range(4):
                rows = rows_of(cx * 8 + 2 * g, cy * 8)
                moved = mm(rows.reshape(256, 64), pick, TN)
                moved = jnp.where(even_lane, moved[0:32], moved[32:64]).astype(BF)
                cut = slice(g * 128, g * 128 + 128)
                ref[first : first + 32, cut] = moved[:, 0:128]
                ref[first + 32 : first + 64, cut] = moved[:, 128:256]


def finish_layer(fo, up, meta, out):
    def rows_of(x, y):
        fine = fo[6 + x : 8 + x, y : y + 8].astype(F32)
        lifted = up[2 + x // 2, 2 + y // 2 : 6 + y // 2]
        lifted = jnp.broadcast_to(lifted[:, None], (4, 2, 16, 64)).reshape(8, 16, 64)
        return (fine + lifted[None]).astype(BF)

    to_bricks(meta, rows_of, out)


def back_conv(first, gw, tb, back):
    for step in range(4):
        value = conv(gw, first + 1 + 2 * step, 2, 1, 16, tb)
        back[2 * step : 2 * step + 2] = value.astype(BF)


def finish_grad(low, high, meta, gfeat):
    def rows_of(x, y):
        ref = low if x < 8 else high
        return ref[x % 8 : x % 8 + 2, y : y + 8]

    to_bricks(meta, rows_of, gfeat)


def unpack(mine, other, gf, gc, gu):
    core = lax.axis_index("gy") % 2
    a, b = mine[...].astype(F32), other[...].astype(F32)
    low, high = jnp.where(core == 0, a, b), jnp.where(core == 0, b, a)
    gf[...] = low[0:32, 0:864]
    gc[0:16] = low[32:48, 0:864]
    gc[16:64] = high[:, 0:864]
    gu[:, 0:32] = low[0:32, 864:896]
    gu[0:16, 32:64] = low[32:48, 864:896]
    gu[16:32, 32:64] = high[0:16, 864:896]


def call(kernel, outs, scratch, args, mib, cost, far=False):
    whole = pl.BlockSpec(memory_space=pltpu.VMEM)
    anywhere = pl.BlockSpec(memory_space=pltpu.HBM)
    return pl.pallas_call(
        kernel,
        out_shape=tuple(jax.ShapeDtypeStruct(shape, kind) for shape, kind in outs),
        in_specs=[anywhere if far else whole] * len(args),
        out_specs=(whole,) * len(outs),
        scratch_shapes=scratch if far else [pltpu.VMEM(shape, kind) for shape, kind in scratch],
        compiler_params=pltpu.CompilerParams(vmem_limit_bytes=mib * 1024 * 1024),
        cost_estimate=pl.CostEstimate(flops=cost, bytes_accessed=2000000, transcendentals=0),
    )(*args)


def step_pairs(dx, dy, wide, across):
    pairs = []
    for x in range(wide):
        for y in range(across):
            if 0 <= x + dx < wide and 0 <= y + dy < across:
                pairs.append((x * across + y, (x + dx) * across + y + dy))
    return pairs


def core_pairs(total):
    return [(i, i ^ 1) for i in range(total)]


def ring_pairs(total, shifts, across):
    pairs = []
    for i in range(total):
        shift = shifts[i & 1]
        q = (i >> shift) & 3
        mate = (q + 1 if q % 2 else q - 1) % 4 if across else q ^ 1
        pairs.append((i, (i & ~(3 << shift)) | (mate << shift)))
    return pairs


def local(features, w_fine, w_coarse, w_up, cotangent, adjacency, parents):
    wide, across = lax.axis_size("gx"), lax.axis_size("gy")
    total = wide * across
    feat = features.reshape(256, 512)
    cot = cotangent.reshape(256, 512)
    up, down, meta = call(
        pack_x,
        [((784, 128), BF), ((784, 128), BF), ((16, 128), BF)],
        [
            pltpu.VMEM((256, 512), BF),
            pltpu.VMEM((256, 512), BF),
            pltpu.SMEM((8,), jnp.int32),
            pltpu.SemaphoreType.DMA((3,)),
        ],
        (parents, feat, cot), 62, 1000000, far=True,
    )
    xm = lax.ppermute(up, AXES, step_pairs(1, 0, wide, across))
    xp = lax.ppermute(down, AXES, step_pairs(-1, 0, wide, across))
    own_fw, own_cd, tf, tb, tc, tg, in_fo, in_pw = call(
        prepare,
        [((16, 16, 16, 128), BF), ((16, 16, 16, 64), BF)]
        + [((384, 192), BF)] * 3
        + [((768, 192), BF), ((12, 12, 16, 64), BF), ((6, 6, 16, 128), BF)],
        [((192, 384), F32), ((192, 384), F32), ((2, 16, 16, 128), F32)],
        (feat, cot, meta, w_fine, w_coarse), 12, 4000000000,
    )
    up, down = call(
        pack_y, [((1456, 128), BF), ((1456, 128), BF)], [],
        (feat, cot, meta, xm, xp), 6, 1000000,
    )
    ym = lax.ppermute(up, AXES, step_pairs(0, 1, wide, across))
    yp = lax.ppermute(down, AXES, step_pairs(0, -1, wide, across))
    mid_fw, mid_cd, mid_fo, mid_pw = call(
        middle,
        [((32, 16, 16, 128), BF), ((32, 16, 16, 64), BF),
         ((16, 12, 16, 64), BF), ((8, 6, 16, 128), BF)],
        [((4, 16, 16, 128), F32)],
        (xm, xp, meta, own_fw, own_cd, tf), 16, 6000000000,
    )
    gw, fo, up, keep, send = call(
        main,
        [((20, 20, 16, 128), BF), ((28, 16, 16, 64), BF), ((12, 12, 16, 64), F32),
         ((48, 896), BF), ((48, 896), BF)],
        [
            ((32, 32, 16, 128), BF),
            ((32, 32, 16, 64), BF),
            ((4, 32, 16, 128), F32),
            ((16, 16, 16, 128), BF),
            ((12, 12, 16, 256), BF),
            ((12, 12, 16, 64), BF),
            ((12, 12, 16, 128), BF),
            ((96, 896), F32),
        ],
        (xm, xp, ym, yp, meta, mid_fw, mid_cd, mid_fo, mid_pw, in_fo, in_pw, tf, tc, tg, w_up),
        36, 20000000000,
    )

    def layer_part(args):
        return call(finish_layer, [((256, 512), BF)], [], args, 8, 2000000000)

    def back_part(first):
        def part(args):
            kernel = functools.partial(back_conv, first)
            return call(kernel, [((8, 16, 16, 64), BF)], [], args, 8, 2000000000)

        return part

    def grad_part(args):
        return call(finish_grad, [((256, 512), BF)], [], args, 8, 2000000000)

    def add(value, pairs, sent=None, part=None, args=()):
        value, args = lax.optimization_barrier((value, args)) if part else (value, args)
        other = lax.ppermute(value if sent is None else sent, AXES, pairs)
        done = part(args)[0] if part else None
        value = (value.astype(F32) + other.astype(F32)).astype(BF)
        return lax.optimization_barrier((value, done)) if part else (value, None)

    value, _ = add(keep, core_pairs(total), send)
    value, out = add(value, ring_pairs(total, (1, 3), False), None, layer_part, (fo, up, meta))
    value, low = add(value, ring_pairs(total, (1, 3), True), None, back_part(0), (gw, tb))
    value, high = add(value, ring_pairs(total, (3, 5), False), None, back_part(8), (gw, tb))
    value, gfeat = add(value, ring_pairs(total, (3, 5), True), None, grad_part, (low, high, meta))
    value, _ = add(value, ring_pairs(total, (5, 1), False))
    value, _ = add(value, ring_pairs(total, (5, 1), True))
    other = lax.ppermute(value, AXES, core_pairs(total))
    gf, gc, gu = call(
        unpack, [((32, 864), F32), ((64, 864), F32), ((32, 64), F32)], [], (value, other), 4, 1000000
    )
    return out.reshape(features.shape), gfeat.reshape(features.shape), gf, gc, gu


def solution(mesh):
    return jax.shard_map(
        local,
        mesh=mesh,
        in_specs=(
            P(("gx", "gy"), None, None),
            P(),
            P(),
            P(),
            P(("gx", "gy"), None, None),
            P(("gx", "gy"), None),
            P(("gx", "gy")),
        ),
        out_specs=(P(("gx", "gy"), None, None), P(("gx", "gy"), None, None), P(), P(), P()),
        check_vma=False,
    )
```

```python
import functools
import math

import jax
import jax.numpy as jnp
from jax import lax
from jax.experimental import pallas as pl
from jax.experimental.pallas import tpu as pltpu
from jax.sharding import PartitionSpec as P

BF = jnp.bfloat16
F32 = jnp.float32
AXES = ("gx", "gy")
NN = (((1,), (0,)), ((), ()))
NT = (((1,), (1,)), ((), ()))
TN = (((0,), (0,)), ((), ()))


def mm(a, b, dims=NN):
    return lax.dot_general(a, b, dims, preferred_element_type=F32)


def halves(value):
    even, odd = value[:, 0:8], value[:, 8:16]
    blank = jnp.zeros((value.shape[0], 1, value.shape[2]), value.dtype)
    odd_before = jnp.concatenate([blank, odd[:, 0:7]], axis=1)
    even_after = jnp.concatenate([even[:, 1:8], blank], axis=1)
    return even, odd, odd_before, even_after


def coarse_window(value):
    even, odd, odd_before, even_after = halves(value)
    blank = jnp.zeros_like(even)
    top = jnp.concatenate([odd_before, even, odd, blank], axis=2)
    low = jnp.concatenate([even, odd, even_after, blank], axis=2)
    return jnp.concatenate([top, low], axis=1)


def fine_window(value):
    even, odd, odd_before, even_after = halves(value)
    top = jnp.concatenate([odd_before[:, :, 32:64], even, odd[:, :, 0:32]], axis=2)
    low = jnp.concatenate([even[:, :, 32:64], odd, even_after[:, :, 0:32]], axis=2)
    return jnp.concatenate([top, low], axis=1)


def place(code):
    return jnp.where(code > 0, code.astype(jnp.int32) * 8 - 8, -100)


def meta_row(ref, base, slot):
    return ref[base : base + 16, 0:128].astype(F32)[slot : slot + 1]


class Either:
    def __init__(self, flag, first, second):
        self.flag, self.first, self.second = flag, first, second

    def __getitem__(self, index):
        return jnp.where(self.flag, self.first[index], self.second[index])


def sides(axis, first, second):
    even = lax.axis_index(axis) % 2 == 0
    return Either(even, second, first), Either(even, first, second)


def by_swap(axis, write, first, second):
    even = lax.axis_index(axis) % 2 == 0

    @pl.when(even)
    def _():
        write(first, second)

    @pl.when(jnp.logical_not(even))
    def _():
        write(second, first)


def roll(value, by):
    return pltpu.roll(value.astype(F32), by, 1).astype(BF)


def source(cx, cy, refs):
    if cy in (1, 2) and cx in (1, 2):
        (own,) = refs
        first = ((cx - 1) * 2 + cy - 1) * 2

        def cut(base, k, g):
            at = base + (first + k) * 32
            return own[at : at + 32, g * 128 : g * 128 + 128]

        return (
            lambda k, g: cut(0, k, g),
            lambda k, g: cut(256, k, g),
            [meta_row(own, 512, first + k) for k in range(2)],
        )
    (ref,) = refs
    if cy in (1, 2):
        first = (cy - 1) * 2
        sender = ((1 if cx == 0 else 0) * 2 + cy - 1) * 2

        def features(k, g):
            at = ((first + k) * 4 + g) * 32
            return ref[at : at + 32]

        def cotangents(k, g):
            at = 512 + ((first + k) * 2 + g % 2) * 32
            return ref[at : at + 32]

        return features, cotangents, [meta_row(ref, 768, sender + k) for k in range(2)]
    sender = ((1, 0, 1, 0)[cx] * 2 + (1 if cy == 0 else 0)) * 2
    base = 1408 + (0, 1, 1, 2)[cx] * 16

    def features(k, g):
        at = ((cx * 2 + k) * 4 + g) * 32
        return ref[at : at + 32]

    def cotangents(k, g):
        at = 1024 + ((max(cx * 2 - 1, 0) + (g // 2 if cx in (1, 2) else 0)) * 2 + k) * 32
        packed = ref[at : at + 32]
        return packed if g % 2 == 0 else roll(packed, 32 if cy == 0 else 96)

    return features, cotangents, [meta_row(ref, base, sender + k) for k in range(2)]


def live_rows(code):
    pair = lax.broadcasted_iota(jnp.int32, (16, 128), 0)
    pair = (pair & 7) * 2 + (pair >> 3)
    live = jnp.zeros((16, 128), F32)
    for value in code:
        live = live + ((pair >> 2) == (value.astype(jnp.int32) - 1)).astype(F32)
    return live


def place_column(cx, cy, refs, fw, cd, x_at, y_at):
    features, cotangents, code = source(cx, cy, refs)
    lane = lax.broadcasted_iota(jnp.int32, (128, 256), 1)
    row = lax.broadcasted_iota(jnp.int32, (128, 256), 0)
    same = (row >> 3) == ((lane & 127) >> 3)
    res = lax.broadcasted_iota(jnp.int32, (32, 256), 1) & 3
    begin = jnp.concatenate([place(value) for value in code], axis=1)
    shift = begin + (lane & 7) - ((row & 7) * 4 - 1)
    pick_even = (same & (shift >= 0) & (shift < 4)).astype(F32).astype(BF)
    pick_odd = (same & (shift >= 2) & (shift < 6)).astype(F32).astype(BF)
    wanted = {0: (2, 3), 1: (0, 1, 2, 3), 2: (0, 1, 2, 3), 3: (0, 1)}[cx]
    for g in range(4):
        f = jnp.concatenate([features(k, g) for k in range(2)], axis=1)
        none = jnp.zeros_like(f)
        fr = [jnp.where(res == i, f, none) for i in range(4)]
        even, odd = [fr[3], fr[0], fr[1], fr[2]], [fr[1], fr[2], fr[3], fr[0]]
        if g in wanted:
            c = jnp.concatenate([cotangents(k, g) for k in range(2)], axis=1)
            cr = [jnp.where(res == i, c, none) for i in range(4)]
            even, odd = even + cr[0:2], odd + cr[2:4]
        lanes = 32 * len(even)
        even = mm(pick_even, jnp.concatenate(even, axis=0), NT).reshape(16, 8, lanes)
        odd = mm(pick_odd, jnp.concatenate(odd, axis=0), NT).reshape(16, 8, lanes)
        both = jnp.concatenate([even, odd], axis=1)
        xs = slice(x_at + 2 * g, x_at + 2 * g + 2)
        ys = slice(y_at, y_at + 8)
        fw[xs, ys] = both[:, :, 0:128].astype(BF).reshape(2, 8, 16, 128)
        if g in wanted:
            cd[xs, ys] = both[:, :, 128:192].astype(BF).reshape(2, 8, 16, 64)
    return code


def pack_x(
    parents_far, feat_far, cot_far, w_fine_far, w_coarse_far,
    first, second, own, weights, parents, sems,
):
    copies = [
        pltpu.make_async_copy(source_ref, target, sems.at[i])
        for i, (source_ref, target) in enumerate(
            (
                (parents_far, parents),
                (feat_far, own.at[0:256]),
                (cot_far, own.at[256:512]),
                (w_fine_far, weights.at[0:32]),
                (w_coarse_far, weights.at[32:96]),
            )
        )
    ]
    for copy in copies:
        copy.start()
    copies[0].wait()
    row = lax.broadcasted_iota(jnp.int32, (16, 128), 0)
    code = jnp.zeros((16, 128), F32)
    for slot in range(8):
        value = parents[slot]
        depth = jnp.where(value >= 0, ((value >> 3) & 1) * 2 + (value & 1) + 1, 0)
        code = jnp.where(row == slot, depth.astype(F32), code)
    code = code.astype(BF)
    own[512:528] = jnp.concatenate([code] * 4, axis=1)
    copies[1].wait()
    copies[2].wait()

    def write(up, down):
        for ref, side in ((up, 1), (down, 0)):
            for slot in range(4):
                at = (side * 4 + slot) * 32
                for g in range(4):
                    to = (slot * 4 + g) * 32
                    ref[to : to + 32] = own[at : at + 32, g * 128 : g * 128 + 128]
                for part in range(2):
                    to = 512 + (slot * 2 + part) * 32
                    lanes = slice((2 * side + part) * 128, (2 * side + part) * 128 + 128)
                    ref[to : to + 32] = own[256 + at : 288 + at, lanes]
            ref[768:784] = code

    by_swap("gx", write, first, second)
    for copy in copies[3:]:
        copy.wait()


def pack_y(own, xa, xb, first, second):
    xm, xp = sides("gx", xa, xb)
    high = (lax.broadcasted_iota(jnp.int32, (32, 128), 1) & 32) != 0

    def write(up, down):
        for ref, side in ((up, 1), (down, 0)):
            pair = 0
            for cx in range(4):
                refs = (xm,) if cx == 0 else (xp,) if cx == 3 else (own,)
                features, cotangents, _ = source(cx, side + 1, refs)
                for k in range(2):
                    for g in range(4):
                        to = ((cx * 2 + k) * 4 + g) * 32
                        ref[to : to + 32] = features(k, g)
                for g in {0: (2,), 1: (0, 2), 2: (0, 2), 3: (0,)}[cx]:
                    for k in range(2):
                        to = 1024 + (pair * 2 + k) * 32
                        here, there = cotangents(k, g), cotangents(k, g + 1)
                        if side == 1:
                            ref[to : to + 32] = jnp.where(high, here, roll(there, 96))
                        else:
                            ref[to : to + 32] = jnp.where(high, roll(there, 32), here)
                    pair += 1
            ref[1408:1424] = xm[768:784]
            ref[1424:1440] = own[512:528, 0:128]
            ref[1440:1456] = xp[768:784]

    by_swap("gy", write, first, second)


def prepare(
    own, weights,
    fw, cd, tf, tb, tc, tg, fo, pw, meta,
    turned_f, turned_c, al,
):
    w_fine, w_coarse = weights.at[0:32], weights.at[32:96]
    meta[...] = own[512:528, 0:128]
    turned_f[...] = jnp.zeros_like(turned_f)
    turned_c[...] = jnp.zeros_like(turned_c)
    tb[...] = jnp.zeros_like(tb)
    tg[...] = jnp.zeros_like(tg)
    for tx in range(3):
        for ty in range(3):
            at = (tx * 3 + ty) * 96
            for zo in range(2):
                to, lanes = (ty * 2 + zo) * 32, tx * 128 + zo * 32
                turned_f[to : to + 32, lanes : lanes + 96] = w_fine[:, at : at + 96].astype(F32)
            turned_c[ty * 64 : ty * 64 + 64, tx * 128 : tx * 128 + 96] = w_coarse[
                :, at : at + 96
            ].astype(F32)
            for tz in range(3):
                at = (((2 - tx) * 3 + 2 - ty) * 3 + 2 - tz) * 32
                for zo in range(2):
                    lanes = (ty * 2 + zo) * 32
                    to = tx * 128 + (tz + zo) * 32
                    tb[to : to + 32, lanes : lanes + 32] = w_fine[:, at : at + 32]
                    to = tx * 256 + tz * 64
                    tg[to : to + 64, lanes : lanes + 32] = w_coarse[:, at : at + 32]
    row = lax.broadcasted_iota(jnp.int32, (384, 384), 0)
    eye = (row == lax.broadcasted_iota(jnp.int32, (384, 384), 1)).astype(F32).astype(BF)
    tf[...] = mm(eye, turned_f[...].astype(BF), NT).astype(BF)
    tc[...] = mm(eye, turned_c[...].astype(BF), NT).astype(BF)
    for cx in (1, 2):
        for cy in (1, 2):
            code = place_column(cx, cy, (own,), fw, cd, cx * 8 - 8, cy * 8 - 8)
            live = live_rows(code)
            for y in range(8):
                al[cx - 1, cy * 8 - 8 + y] = live
    for at in range(6):
        value = conv(fw, 1 + 2 * at, 2, 1, 12, tf)
        fine = (value * al[(2 + 2 * at) // 8, 2:14, :, 0:64][None]).astype(BF)
        pw[at] = pool(fine)
        fo[2 * at : 2 * at + 2] = fine


def conv_rows(ref, x_first, planes, y_first, width):
    rows = planes * (width + 2) * 16
    return jnp.concatenate(
        [
            ref[pl.ds(x_first + tap, planes), y_first : y_first + width + 2].reshape(
                rows, ref.shape[3]
            )
            for tap in range(3)
        ],
        axis=1,
    )


def conv_taps(wide, width):
    return (
        wide[:, 0:width, :, 0:64]
        + wide[:, 1 : width + 1, :, 64:128]
        + wide[:, 2 : width + 2, :, 128:192]
    )


def conv(ref, x_first, planes, y_first, width, weight):
    rows = conv_rows(ref, x_first, planes, y_first, width)
    return conv_taps(mm(rows, weight[...]).reshape(planes, width + 2, 16, 192), width)


def pool(fine):
    rows = fine.shape[1] // 2
    pooled = fine.astype(F32)
    pooled = (pooled[0] + pooled[1]).reshape(rows, 2, 16, 64)
    pooled = pooled[:, 0] + pooled[:, 1]
    return coarse_window((pooled[:, :, 0:32] + pooled[:, :, 32:64]) * 0.125).astype(BF)


def middle(xa, xb, meta, own_fw, own_cd, tf, fw, cd, fo, pw, al):
    xm, xp = sides("gx", xa, xb)
    fw[8:24] = own_fw[...]
    cd[8:24] = own_cd[...]
    for cx in range(4):
        for cy in (1, 2):
            if cx in (0, 3):
                refs = (xm,) if cx == 0 else (xp,)
                code = place_column(cx, cy, refs, fw, cd, cx * 8, cy * 8 - 8)
            else:
                code = [meta_row(meta, 0, ((cx - 1) * 2 + cy - 1) * 2 + k) for k in range(2)]
            live = live_rows(code)
            for y in range(8):
                al[cx, cy * 8 - 8 + y] = live

    for order, at in enumerate((0, 1, 2, 3, 10, 11, 12, 13)):
        value = conv(fw, 1 + 2 * at, 2, 1, 12, tf)
        fine = (value * al[(2 + 2 * at) // 8, 2:14, :, 0:64][None]).astype(BF)
        pw[order] = pool(fine)
        fo[2 * order : 2 * order + 2] = fine


def main(
    xa, xb, ya, yb, meta, mid_fw, mid_cd, mid_fo, mid_pw, in_fo, in_pw, tf, tc, tg, w_up,
    gw, fo, act, keep, send,
    fw, cd, al, pw, cg, gs, sums,
):
    xm, xp = sides("gx", xa, xb)
    ym, yp = sides("gy", ya, yb)
    fw[:, 8:24] = mid_fw[...]
    cd[:, 8:24] = mid_cd[...]
    fo[0:8, 2:14] = mid_fo[0:8]
    fo[8:20, 2:14] = in_fo[...]
    fo[20:28, 2:14] = mid_fo[8:16]
    pw[1:5, 5:11] = mid_pw[0:4]
    pw[5:11, 5:11] = in_pw[...]
    pw[11:15, 5:11] = mid_pw[4:8]
    for cx in range(4):
        for cy in range(4):
            if cy in (0, 3):
                refs = (ym,) if cy == 0 else (yp,)
                code = place_column(cx, cy, refs, fw, cd, cx * 8, cy * 8)
            else:
                if cx in (0, 3):
                    code = source(cx, cy, (xm,) if cx == 0 else (xp,))[2]
                else:
                    code = [meta_row(meta, 0, ((cx - 1) * 2 + cy - 1) * 2 + k) for k in range(2)]
            live = live_rows(code)
            for y in range(8):
                al[cx, cy * 8 + y] = live

    for step in range(14):
        rows = [conv_rows(fw, 1 + 2 * step, 2, first, 8) for first in (1, 21)]
        wide = mm(jnp.concatenate(rows, axis=0), tf[...]).reshape(2, 2, 10, 16, 192)
        column = (2 + 2 * step) // 8
        first = (conv_taps(wide[0], 8) * al[column, 2:10, :, 0:64][None]).astype(BF)
        second = (conv_taps(wide[1], 8) * al[column, 22:30, :, 0:64][None]).astype(BF)
        pw[1 + step, 1:5] = pool(first)
        pw[1 + step, 11:15] = pool(second)
        fo[2 * step : 2 * step + 2, 0:2] = first[:, 6:8]
        fo[2 * step : 2 * step + 2, 14:16] = second[:, 0:2]

    four = jnp.concatenate([w_up[...]] * 4, axis=0)
    for x in range(0, 12, 4):
        pre = conv(pw, 1 + x, 4, 1, 12, tc)
        sig = 1.0 / (1.0 + jnp.exp(-pre))
        act[x : x + 4] = (pre * sig).astype(BF)
        pair = cd[4 + 2 * x : 4 + 2 * x + 2 * 4, 4:28].astype(F32).reshape(4, 2, 24, 16, 64)
        pair = (pair[:, 0] + pair[:, 1]).reshape(4, 12, 2, 16, 64)
        pair = pair[:, :, 0] + pair[:, :, 1]
        high = pair.astype(BF)
        low = (pair - high.astype(F32)).astype(BF)
        split = jnp.concatenate([high, low], axis=3)
        gs[x : x + 4] = split
        back = mm(split.reshape(4 * 192, 128), four).reshape(4, 12, 16, 64)
        grad = back * sig * (1.0 + pre * (1.0 - sig))
        window = coarse_window(grad.reshape(4 * 12, 16, 64)).astype(BF)
        cg[x : x + 4] = window.reshape(4, 12, 16, 256)

    for first in range(0, 10, 1):
        pooled_grad = conv(cg, first, 1, 0, 10, tg) * 0.125
        for plane in range(1):
            spread = jnp.broadcast_to(pooled_grad[plane][:, None], (10, 2, 16, 64))
            spread = spread.reshape(20, 16, 64)
            for half in range(2):
                at = 2 * (first + plane) + half
                seed = cd[6 + at, 6:26].astype(F32)
                grad = (seed + spread) * al[(6 + at) // 8, 6:26, :, 0:64]
                gw[at] = fine_window(grad).astype(BF)

    total = jnp.zeros((64, 1152), F32)
    for x in range(0, 16, 2):
        grad = gw[2 + x : 4 + x, 2:18].reshape(512, 128)[:, 32:96]
        taps = [
            fw[7 + x + tap // 3 : 9 + x + tap // 3, 7 + tap % 3 : 23 + tap % 3].reshape(512, 128)
            for tap in range(9)
        ]
        total = total + mm(grad, jnp.concatenate(taps, axis=1), TN)
    fine_scale = 1.0 / math.sqrt(524288)
    coarse_scale = 1.0 / math.sqrt(131072)
    sums[...] = jnp.zeros_like(sums)
    for tap in range(9):
        at = tap * 128
        term = total[0:32, at : at + 96] + total[32:64, at + 32 : at + 128]
        sums[0:32, tap * 96 : tap * 96 + 96] = term * fine_scale

    total = jnp.zeros((64, 1152), F32)
    total_up = jnp.zeros((128, 64), F32)
    for x in (0, 4):
        grad = cg[2 + x : 6 + x, 2:10].reshape(512, 256)[:, 64:128]
        taps = [
            pw[3 + x + tap // 3 : 7 + x + tap // 3, 3 + tap % 3 : 11 + tap % 3].reshape(512, 128)
            for tap in range(9)
        ]
        total = total + mm(grad, jnp.concatenate(taps, axis=1), TN)
        silu = act[2 + x : 6 + x, 2:10].reshape(512, 64)
        total_up = total_up + mm(gs[2 + x : 6 + x, 2:10].reshape(512, 128), silu, TN)
    for tap in range(9):
        at = tap * 128
        sums[32:96, tap * 96 : tap * 96 + 96] = total[:, at : at + 96] * coarse_scale
    total_up = total_up[0:32] + total_up[32:64] + total_up[64:96] + total_up[96:128]
    sums[0:32, 864:896] = total_up[:, 0:32] * coarse_scale
    sums[32:64, 864:896] = total_up[:, 32:64] * coarse_scale
    core = lax.axis_index("gy") % 2
    low, high = sums[0:48], sums[48:96]
    keep[...] = jnp.where(core == 0, low, high).astype(BF)
    send[...] = jnp.where(core == 0, high, low).astype(BF)


def to_bricks(meta, rows_of, ref):
    lane = lax.broadcasted_iota(jnp.int32, (256, 256), 1)
    row = lax.broadcasted_iota(jnp.int32, (256, 256), 0)
    same = (row >> 4) == ((lane & 127) >> 3)
    target = (row & 7) * 2 + ((row >> 3) & 1)
    even_lane = (lax.broadcasted_iota(jnp.int32, (32, 256), 1) & 1) == 0
    for cx in range(2):
        for cy in range(2):
            code = [meta_row(meta, 0, (cx * 2 + cy) * 2 + k) for k in range(2)]
            begin = jnp.concatenate([place(value) for value in code], axis=1)
            pick = (same & (((begin + (lane & 7)) >> 1) == target)).astype(F32).astype(BF)
            first = (cx * 2 + cy) * 64
            for g in range(4):
                rows = rows_of(cx * 8 + 2 * g, cy * 8)
                moved = mm(rows.reshape(256, 64), pick, TN)
                moved = jnp.where(even_lane, moved[0:32], moved[32:64]).astype(BF)
                cut = slice(g * 128, g * 128 + 128)
                ref[first : first + 32, cut] = moved[:, 0:128]
                ref[first + 32 : first + 64, cut] = moved[:, 128:256]


def finish_layer(fo, act, w_up, meta, out):
    twice = jnp.concatenate([w_up[...]] * 2, axis=0)
    up = mm(act[2:10, 2:10].reshape(1024, 64), twice, NT).reshape(8, 8, 16, 64)

    def rows_of(x, y):
        fine = fo[6 + x : 8 + x, y : y + 8].astype(F32)
        lifted = up[x // 2, y // 2 : 4 + y // 2]
        lifted = jnp.broadcast_to(lifted[:, None], (4, 2, 16, 64)).reshape(8, 16, 64)
        return (fine + lifted[None]).astype(BF)

    to_bricks(meta, rows_of, out)


def back_conv(first, gw, tb, back):
    for step in range(4):
        value = conv(gw, first + 1 + 2 * step, 2, 1, 16, tb)
        back[2 * step : 2 * step + 2] = value.astype(BF)


def finish_grad(low, high, meta, gfeat):
    def rows_of(x, y):
        ref = low if x < 8 else high
        return ref[x % 8 : x % 8 + 2, y : y + 8]

    to_bricks(meta, rows_of, gfeat)


def unpack(mine, other, gf, gc, gu):
    core = lax.axis_index("gy") % 2
    a, b = mine[...].astype(F32), other[...].astype(F32)
    low, high = jnp.where(core == 0, a, b), jnp.where(core == 0, b, a)
    gf[...] = low[0:32, 0:864]
    gc[0:16] = low[32:48, 0:864]
    gc[16:64] = high[:, 0:864]
    gu[:, 0:32] = low[0:32, 864:896]
    gu[0:16, 32:64] = low[32:48, 864:896]
    gu[16:32, 32:64] = high[0:16, 864:896]


def call(kernel, outs, scratch, args, mib, cost, far=False):
    whole = pl.BlockSpec(memory_space=pltpu.VMEM)
    anywhere = pl.BlockSpec(memory_space=pltpu.HBM)
    return pl.pallas_call(
        kernel,
        out_shape=tuple(jax.ShapeDtypeStruct(shape, kind) for shape, kind in outs),
        in_specs=[anywhere if far else whole] * len(args),
        out_specs=(whole,) * len(outs),
        scratch_shapes=scratch if far else [pltpu.VMEM(shape, kind) for shape, kind in scratch],
        compiler_params=pltpu.CompilerParams(vmem_limit_bytes=mib * 1024 * 1024),
        cost_estimate=pl.CostEstimate(flops=cost, bytes_accessed=2000000, transcendentals=0),
    )(*args)


def swap_pairs(length, first):
    pairs = []
    for i in range(first, length - 1, 2):
        pairs += [(i, i + 1), (i + 1, i)]
    return pairs


def core_pairs(total):
    return [(i, i ^ 1) for i in range(total)]


def ring_pairs(total, shifts, across):
    pairs = []
    for i in range(total):
        shift = shifts[i & 1]
        q = (i >> shift) & 3
        mate = (q + 1 if q % 2 else q - 1) % 4 if across else q ^ 1
        pairs.append((i, (i & ~(3 << shift)) | (mate << shift)))
    return pairs


def local(features, w_fine, w_coarse, w_up, cotangent, adjacency, parents):
    wide, across = lax.axis_size("gx"), lax.axis_size("gy")
    total = wide * across
    feat = features.reshape(256, 512)
    cot = cotangent.reshape(256, 512)
    first, second, own, weights = call(
        pack_x,
        [((784, 128), BF), ((784, 128), BF), ((528, 512), BF), ((96, 864), BF)],
        [pltpu.SMEM((8,), jnp.int32), pltpu.SemaphoreType.DMA((5,))],
        (parents, feat, cot, w_fine, w_coarse), 62, 1000000, far=True,
    )
    xa = lax.ppermute(first, "gx", swap_pairs(wide, 0))
    xb = lax.ppermute(second, "gx", swap_pairs(wide, 1))
    own_fw, own_cd, tf, tb, tc, tg, in_fo, in_pw, meta = call(
        prepare,
        [((16, 16, 16, 128), BF), ((16, 16, 16, 64), BF)]
        + [((384, 192), BF)] * 3
        + [((768, 192), BF), ((12, 12, 16, 64), BF), ((6, 6, 16, 128), BF), ((16, 128), BF)],
        [((192, 384), F32), ((192, 384), F32), ((2, 16, 16, 128), F32)],
        (own, weights), 12, 4000000000,
    )
    first, second = call(
        pack_y, [((1456, 128), BF), ((1456, 128), BF)], [], (own, xa, xb), 6, 1000000,
    )
    ya = lax.ppermute(first, "gy", swap_pairs(across, 0))
    yb = lax.ppermute(second, "gy", swap_pairs(across, 1))
    mid_fw, mid_cd, mid_fo, mid_pw = call(
        middle,
        [((32, 16, 16, 128), BF), ((32, 16, 16, 64), BF),
         ((16, 12, 16, 64), BF), ((8, 6, 16, 128), BF)],
        [((4, 16, 16, 128), F32)],
        (xa, xb, meta, own_fw, own_cd, tf), 16, 6000000000,
    )
    gw, fo, act, keep, send = call(
        main,
        [((20, 20, 16, 128), BF), ((28, 16, 16, 64), BF), ((12, 12, 16, 64), BF),
         ((48, 896), BF), ((48, 896), BF)],
        [
            ((32, 32, 16, 128), BF),
            ((32, 32, 16, 64), BF),
            ((4, 32, 16, 128), F32),
            ((16, 16, 16, 128), BF),
            ((12, 12, 16, 256), BF),
            ((12, 12, 16, 128), BF),
            ((96, 896), F32),
        ],
        (xa, xb, ya, yb, meta, mid_fw, mid_cd, mid_fo, mid_pw, in_fo, in_pw, tf, tc, tg, w_up),
        36, 20000000000,
    )

    def layer_part(args):
        return call(finish_layer, [((256, 512), BF)], [], args, 8, 2000000000)

    def back_part(first):
        def part(args):
            kernel = functools.partial(back_conv, first)
            return call(kernel, [((8, 16, 16, 64), BF)], [], args, 8, 2000000000)

        return part

    def grad_part(args):
        return call(finish_grad, [((256, 512), BF)], [], args, 8, 2000000000)

    def add(value, pairs, sent=None, part=None, args=()):
        value, args = lax.optimization_barrier((value, args)) if part else (value, args)
        other = lax.ppermute(value if sent is None else sent, AXES, pairs)
        done = part(args)[0] if part else None
        value = (value.astype(F32) + other.astype(F32)).astype(BF)
        return lax.optimization_barrier((value, done)) if part else (value, None)

    value, _ = add(keep, core_pairs(total), send)
    value, out = add(value, ring_pairs(total, (1, 3), False), None, layer_part, (fo, act, w_up, meta))
    value, low = add(value, ring_pairs(total, (1, 3), True), None, back_part(0), (gw, tb))
    value, high = add(value, ring_pairs(total, (3, 5), False), None, back_part(8), (gw, tb))
    value, gfeat = add(value, ring_pairs(total, (3, 5), True), None, grad_part, (low, high, meta))
    value, _ = add(value, ring_pairs(total, (5, 1), False))
    value, _ = add(value, ring_pairs(total, (5, 1), True))
    other = lax.ppermute(value, AXES, core_pairs(total))
    gf, gc, gu = call(
        unpack, [((32, 864), F32), ((64, 864), F32), ((32, 64), F32)], [], (value, other), 4, 1000000
    )
    return out.reshape(features.shape), gfeat.reshape(features.shape), gf, gc, gu


def solution(mesh):
    return jax.shard_map(
        local,
        mesh=mesh,
        in_specs=(
            P(("gx", "gy"), None, None),
            P(),
            P(),
            P(),
            P(("gx", "gy"), None, None),
            P(("gx", "gy"), None),
            P(("gx", "gy")),
        ),
        out_specs=(P(("gx", "gy"), None, None), P(("gx", "gy"), None, None), P(), P(), P()),
        check_vma=False,
    )
```

```python
import functools
import math

import jax
import jax.numpy as jnp
from jax import lax
from jax.experimental import pallas as pl
from jax.experimental.pallas import tpu as pltpu
from jax.sharding import PartitionSpec as P

BF = jnp.bfloat16
F32 = jnp.float32
AXES = ("gx", "gy")
NN = (((1,), (0,)), ((), ()))
NT = (((1,), (1,)), ((), ()))
TN = (((0,), (0,)), ((), ()))


def mm(a, b, dims=NN):
    return lax.dot_general(a, b, dims, preferred_element_type=F32)


def halves(value):
    even, odd = value[:, 0:8], value[:, 8:16]
    blank = jnp.zeros((value.shape[0], 1, value.shape[2]), value.dtype)
    odd_before = jnp.concatenate([blank, odd[:, 0:7]], axis=1)
    even_after = jnp.concatenate([even[:, 1:8], blank], axis=1)
    return even, odd, odd_before, even_after


def coarse_window(value):
    even, odd, odd_before, even_after = halves(value)
    blank = jnp.zeros_like(even)
    top = jnp.concatenate([odd_before, even, odd, blank], axis=2)
    low = jnp.concatenate([even, odd, even_after, blank], axis=2)
    return jnp.concatenate([top, low], axis=1)


def fine_window(value):
    even, odd, odd_before, even_after = halves(value)
    top = jnp.concatenate([odd_before[:, :, 32:64], even, odd[:, :, 0:32]], axis=2)
    low = jnp.concatenate([even[:, :, 32:64], odd, even_after[:, :, 0:32]], axis=2)
    return jnp.concatenate([top, low], axis=1)


def place(code):
    return jnp.where(code > 0, code.astype(jnp.int32) * 8 - 8, -100)


def meta_row(ref, base, slot):
    return ref[base : base + 16, 0:128].astype(F32)[slot : slot + 1]


class Either:
    def __init__(self, flag, first, second):
        self.flag, self.first, self.second = flag, first, second

    def __getitem__(self, index):
        return jnp.where(self.flag, self.first[index], self.second[index])


def sides(axis, first, second):
    even = lax.axis_index(axis) % 2 == 0
    return Either(even, second, first), Either(even, first, second)


def by_swap(axis, write, first, second):
    even = lax.axis_index(axis) % 2 == 0

    @pl.when(even)
    def _():
        write(first, second)

    @pl.when(jnp.logical_not(even))
    def _():
        write(second, first)


def roll(value, by):
    return pltpu.roll(value.astype(F32), by, 1).astype(BF)


def source(cx, cy, refs):
    if cy in (1, 2) and cx in (1, 2):
        (own,) = refs
        first = ((cx - 1) * 2 + cy - 1) * 2

        def cut(base, k, g):
            at = base + (first + k) * 32
            return own[at : at + 32, g * 128 : g * 128 + 128]

        return (
            lambda k, g: cut(0, k, g),
            lambda k, g: cut(256, k, g),
            [meta_row(own, 512, first + k) for k in range(2)],
        )
    (ref,) = refs
    if cy in (1, 2):
        first = (cy - 1) * 2
        sender = ((1 if cx == 0 else 0) * 2 + cy - 1) * 2

        def features(k, g):
            at = ((first + k) * 4 + g) * 32
            return ref[at : at + 32]

        def cotangents(k, g):
            at = 512 + ((first + k) * 2 + g % 2) * 32
            return ref[at : at + 32]

        return features, cotangents, [meta_row(ref, 768, sender + k) for k in range(2)]
    sender = ((1, 0, 1, 0)[cx] * 2 + (1 if cy == 0 else 0)) * 2
    corner = cx in (0, 3)
    place_in = cx // 3 if corner else cx - 1
    base = 640 + place_in * 16 if corner else 768

    def features(k, g):
        at = ((place_in * 2 + k) * 4 + g) * 32
        return ref[at : at + 32]

    def cotangents(k, g):
        at = 512 + ((place_in if corner else place_in * 2 + g // 2) * 2 + k) * 32
        packed = ref[at : at + 32]
        return packed if g % 2 == 0 else roll(packed, 32 if cy == 0 else 96)

    return features, cotangents, [meta_row(ref, base, sender + k) for k in range(2)]


def half_rows(side, here, there):
    high = (lax.broadcasted_iota(jnp.int32, (32, 128), 1) & 32) != 0
    if side == 1:
        return jnp.where(high, here, roll(there, 96))
    return jnp.where(high, roll(there, 32), here)


def live_rows(code):
    pair = lax.broadcasted_iota(jnp.int32, (16, 128), 0)
    pair = (pair & 7) * 2 + (pair >> 3)
    live = jnp.zeros((16, 128), F32)
    for value in code:
        live = live + ((pair >> 2) == (value.astype(jnp.int32) - 1)).astype(F32)
    return live


def place_column(cx, cy, refs, fw, cd, x_at, y_at):
    features, cotangents, code = source(cx, cy, refs)
    lane = lax.broadcasted_iota(jnp.int32, (128, 256), 1)
    row = lax.broadcasted_iota(jnp.int32, (128, 256), 0)
    same = (row >> 3) == ((lane & 127) >> 3)
    res = lax.broadcasted_iota(jnp.int32, (32, 256), 1) & 3
    begin = jnp.concatenate([place(value) for value in code], axis=1)
    shift = begin + (lane & 7) - ((row & 7) * 4 - 1)
    pick_even = (same & (shift >= 0) & (shift < 4)).astype(F32).astype(BF)
    pick_odd = (same & (shift >= 2) & (shift < 6)).astype(F32).astype(BF)
    wanted = {0: (2, 3), 1: (0, 1, 2, 3), 2: (0, 1, 2, 3), 3: (0, 1)}[cx]
    for g in range(4):
        f = jnp.concatenate([features(k, g) for k in range(2)], axis=1)
        none = jnp.zeros_like(f)
        fr = [jnp.where(res == i, f, none) for i in range(4)]
        even, odd = [fr[3], fr[0], fr[1], fr[2]], [fr[1], fr[2], fr[3], fr[0]]
        if g in wanted:
            c = jnp.concatenate([cotangents(k, g) for k in range(2)], axis=1)
            cr = [jnp.where(res == i, c, none) for i in range(4)]
            even, odd = even + cr[0:2], odd + cr[2:4]
        lanes = 32 * len(even)
        even = mm(pick_even, jnp.concatenate(even, axis=0), NT).reshape(16, 8, lanes)
        odd = mm(pick_odd, jnp.concatenate(odd, axis=0), NT).reshape(16, 8, lanes)
        both = jnp.concatenate([even, odd], axis=1)
        xs = slice(x_at + 2 * g, x_at + 2 * g + 2)
        ys = slice(y_at, y_at + 8)
        fw[xs, ys] = both[:, :, 0:128].astype(BF).reshape(2, 8, 16, 128)
        if g in wanted:
            cd[xs, ys] = both[:, :, 128:192].astype(BF).reshape(2, 8, 16, 64)
    return code


def pack_own(
    parents_far, feat_far, cot_far, w_fine_far, w_coarse_far,
    first, second, first_y, second_y, own, w_fine, w_coarse, parents, sems,
):
    copies = [
        pltpu.make_async_copy(source_ref, target, sems.at[i])
        for i, (source_ref, target) in enumerate(
            (
                (parents_far, parents),
                (feat_far, own.at[0:256]),
                (cot_far, own.at[256:512]),
                (w_fine_far, w_fine),
                (w_coarse_far, w_coarse),
            )
        )
    ]
    for copy in copies:
        copy.start()
    copies[0].wait()
    row = lax.broadcasted_iota(jnp.int32, (16, 128), 0)
    code = jnp.zeros((16, 128), F32)
    for slot in range(8):
        value = parents[slot]
        depth = jnp.where(value >= 0, ((value >> 3) & 1) * 2 + (value & 1) + 1, 0)
        code = jnp.where(row == slot, depth.astype(F32), code)
    code = code.astype(BF)
    own[512:528] = jnp.concatenate([code] * 4, axis=1)
    copies[1].wait()
    copies[2].wait()

    def write(up, down):
        for ref, side in ((up, 1), (down, 0)):
            for slot in range(4):
                at = (side * 4 + slot) * 32
                for g in range(4):
                    to = (slot * 4 + g) * 32
                    ref[to : to + 32] = own[at : at + 32, g * 128 : g * 128 + 128]
                for part in range(2):
                    to = 512 + (slot * 2 + part) * 32
                    lanes = slice((2 * side + part) * 128, (2 * side + part) * 128 + 128)
                    ref[to : to + 32] = own[256 + at : 288 + at, lanes]
            ref[768:784] = code

    def write_y(up, down):
        for ref, side in ((up, 1), (down, 0)):
            for cx in (1, 2):
                features, cotangents, _ = source(cx, side + 1, (own,))
                for k in range(2):
                    for g in range(4):
                        to = (((cx - 1) * 2 + k) * 4 + g) * 32
                        ref[to : to + 32] = features(k, g)
                    for g in (0, 2):
                        to = 512 + (((cx - 1) * 2 + g // 2) * 2 + k) * 32
                        ref[to : to + 32] = half_rows(side, cotangents(k, g), cotangents(k, g + 1))
            ref[768:784] = code

    by_swap("gx", write, first, second)
    by_swap("gy", write_y, first_y, second_y)
    for copy in copies[3:]:
        copy.wait()
    for ref, at in ((w_fine, 528), (w_coarse, 560)):
        rows = ref.shape[0]
        own[at : at + rows] = ref[:, 0:512]
        own[at + 96 : at + 96 + rows, 0:352] = ref[:, 512:864]


def pack_corners(xa, xb, first, second):
    xm, xp = sides("gx", xa, xb)

    def write(up, down):
        for ref, side in ((up, 1), (down, 0)):
            for at, (cx, came) in enumerate(((0, xm), (3, xp))):
                features, cotangents, _ = source(cx, side + 1, (came,))
                for k in range(2):
                    for g in range(4):
                        to = ((at * 2 + k) * 4 + g) * 32
                        ref[to : to + 32] = features(k, g)
                    to = 512 + (at * 2 + k) * 32
                    ref[to : to + 32] = half_rows(side, cotangents(k, 0), cotangents(k, 1))
                ref[640 + at * 16 : 656 + at * 16] = came[768:784]

    by_swap("gy", write, first, second)


def prepare(
    own,
    fw, cd, tf, tb, tc, tg, fo, pw, meta,
    turned_f, turned_c, al,
):
    w_fine = jnp.concatenate([own[528:560], own[624:656, 0:352]], axis=1)
    w_coarse = jnp.concatenate([own[560:624], own[656:720, 0:352]], axis=1)
    meta[...] = own[512:528, 0:128]
    turned_f[...] = jnp.zeros_like(turned_f)
    turned_c[...] = jnp.zeros_like(turned_c)
    tb[...] = jnp.zeros_like(tb)
    tg[...] = jnp.zeros_like(tg)
    for tx in range(3):
        for ty in range(3):
            at = (tx * 3 + ty) * 96
            for zo in range(2):
                to, lanes = (ty * 2 + zo) * 32, tx * 128 + zo * 32
                turned_f[to : to + 32, lanes : lanes + 96] = w_fine[:, at : at + 96].astype(F32)
            turned_c[ty * 64 : ty * 64 + 64, tx * 128 : tx * 128 + 96] = w_coarse[
                :, at : at + 96
            ].astype(F32)
            for tz in range(3):
                at = (((2 - tx) * 3 + 2 - ty) * 3 + 2 - tz) * 32
                for zo in range(2):
                    lanes = (ty * 2 + zo) * 32
                    to = tx * 128 + (tz + zo) * 32
                    tb[to : to + 32, lanes : lanes + 32] = w_fine[:, at : at + 32]
                    to = tx * 256 + tz * 64
                    tg[to : to + 64, lanes : lanes + 32] = w_coarse[:, at : at + 32]
    row = lax.broadcasted_iota(jnp.int32, (384, 384), 0)
    eye = (row == lax.broadcasted_iota(jnp.int32, (384, 384), 1)).astype(F32).astype(BF)
    tf[...] = mm(eye, turned_f[...].astype(BF), NT).astype(BF)
    tc[...] = mm(eye, turned_c[...].astype(BF), NT).astype(BF)
    for cx in (1, 2):
        for cy in (1, 2):
            code = place_column(cx, cy, (own,), fw, cd, cx * 8 - 8, cy * 8 - 8)
            live = live_rows(code)
            for y in range(8):
                al[cx - 1, cy * 8 - 8 + y] = live
    for at in range(6):
        value = conv(fw, 1 + 2 * at, 2, 1, 12, tf)
        fine = (value * al[(2 + 2 * at) // 8, 2:14, :, 0:64][None]).astype(BF)
        pw[at] = pool(fine)
        fo[2 * at : 2 * at + 2] = fine


def conv_rows(ref, x_first, planes, y_first, width):
    rows = planes * (width + 2) * 16
    return jnp.concatenate(
        [
            ref[pl.ds(x_first + tap, planes), y_first : y_first + width + 2].reshape(
                rows, ref.shape[3]
            )
            for tap in range(3)
        ],
        axis=1,
    )


def conv_taps(wide, width):
    return (
        wide[:, 0:width, :, 0:64]
        + wide[:, 1 : width + 1, :, 64:128]
        + wide[:, 2 : width + 2, :, 128:192]
    )


def conv(ref, x_first, planes, y_first, width, weight):
    rows = conv_rows(ref, x_first, planes, y_first, width)
    return conv_taps(mm(rows, weight[...]).reshape(planes, width + 2, 16, 192), width)


def pool(fine):
    rows = fine.shape[1] // 2
    pooled = fine.astype(F32)
    pooled = (pooled[0] + pooled[1]).reshape(rows, 2, 16, 64)
    pooled = pooled[:, 0] + pooled[:, 1]
    return coarse_window((pooled[:, :, 0:32] + pooled[:, :, 32:64]) * 0.125).astype(BF)


def middle(xa, xb, oa, ob, meta, own_fw, own_cd, tf, fw, cd, fo, pw, al):
    xm, xp = sides("gx", xa, xb)
    om, op = sides("gy", oa, ob)
    fw[8:24, 8:24] = own_fw[...]
    cd[8:24, 8:24] = own_cd[...]
    for cx in (1, 2):
        place_column(cx, 0, (om,), fw, cd, cx * 8, 0)
        place_column(cx, 3, (op,), fw, cd, cx * 8, 24)
    for cx in range(4):
        for cy in (1, 2):
            if cx in (0, 3):
                refs = (xm,) if cx == 0 else (xp,)
                code = place_column(cx, cy, refs, fw, cd, cx * 8, cy * 8)
            else:
                code = [meta_row(meta, 0, ((cx - 1) * 2 + cy - 1) * 2 + k) for k in range(2)]
            live = live_rows(code)
            for y in range(8):
                al[cx, cy * 8 - 8 + y] = live

    for order, at in enumerate((0, 1, 2, 3, 10, 11, 12, 13)):
        value = conv(fw, 1 + 2 * at, 2, 9, 12, tf)
        fine = (value * al[(2 + 2 * at) // 8, 2:14, :, 0:64][None]).astype(BF)
        pw[order] = pool(fine)
        fo[2 * order : 2 * order + 2] = fine


def main(
    xa, xb, oa, ob, ya, yb, meta, mid_fw, mid_cd, mid_fo, mid_pw, in_fo, in_pw, tf, tc, tg, w_up,
    gw, fo, act, keep, send,
    fw, cd, al, pw, cg, gs, sums,
):
    xm, xp = sides("gx", xa, xb)
    om, op = sides("gy", oa, ob)
    ym, yp = sides("gy", ya, yb)
    for ref, came in ((fw, mid_fw), (cd, mid_cd)):
        ref[:, 8:24] = came[:, 8:24]
        ref[8:24, 0:8] = came[8:24, 0:8]
        ref[8:24, 24:32] = came[8:24, 24:32]
    fo[0:8, 2:14] = mid_fo[0:8]
    fo[8:20, 2:14] = in_fo[...]
    fo[20:28, 2:14] = mid_fo[8:16]
    pw[1:5, 5:11] = mid_pw[0:4]
    pw[5:11, 5:11] = in_pw[...]
    pw[11:15, 5:11] = mid_pw[4:8]
    for cx in range(4):
        for cy in range(4):
            if cy in (0, 3):
                if cx in (0, 3):
                    refs = (ym,) if cy == 0 else (yp,)
                    code = place_column(cx, cy, refs, fw, cd, cx * 8, cy * 8)
                else:
                    code = source(cx, cy, (om,) if cy == 0 else (op,))[2]
            else:
                if cx in (0, 3):
                    code = source(cx, cy, (xm,) if cx == 0 else (xp,))[2]
                else:
                    code = [meta_row(meta, 0, ((cx - 1) * 2 + cy - 1) * 2 + k) for k in range(2)]
            live = live_rows(code)
            for y in range(8):
                al[cx, cy * 8 + y] = live

    for step in range(14):
        rows = [conv_rows(fw, 1 + 2 * step, 2, first, 8) for first in (1, 21)]
        wide = mm(jnp.concatenate(rows, axis=0), tf[...]).reshape(2, 2, 10, 16, 192)
        column = (2 + 2 * step) // 8
        first = (conv_taps(wide[0], 8) * al[column, 2:10, :, 0:64][None]).astype(BF)
        second = (conv_taps(wide[1], 8) * al[column, 22:30, :, 0:64][None]).astype(BF)
        pw[1 + step, 1:5] = pool(first)
        pw[1 + step, 11:15] = pool(second)
        fo[2 * step : 2 * step + 2, 0:2] = first[:, 6:8]
        fo[2 * step : 2 * step + 2, 14:16] = second[:, 0:2]

    four = jnp.concatenate([w_up[...]] * 4, axis=0)
    for x in range(0, 12, 4):
        pre = conv(pw, 1 + x, 4, 1, 12, tc)
        sig = 1.0 / (1.0 + jnp.exp(-pre))
        act[x : x + 4] = (pre * sig).astype(BF)
        pair = cd[4 + 2 * x : 4 + 2 * x + 2 * 4, 4:28].astype(F32).reshape(4, 2, 24, 16, 64)
        pair = (pair[:, 0] + pair[:, 1]).reshape(4, 12, 2, 16, 64)
        pair = pair[:, :, 0] + pair[:, :, 1]
        high = pair.astype(BF)
        low = (pair - high.astype(F32)).astype(BF)
        split = jnp.concatenate([high, low], axis=3)
        gs[x : x + 4] = split
        back = mm(split.reshape(4 * 192, 128), four).reshape(4, 12, 16, 64)
        grad = back * sig * (1.0 + pre * (1.0 - sig))
        window = coarse_window(grad.reshape(4 * 12, 16, 64)).astype(BF)
        cg[x : x + 4] = window.reshape(4, 12, 16, 256)

    for first in range(0, 10, 1):
        pooled_grad = conv(cg, first, 1, 0, 10, tg) * 0.125
        for plane in range(1):
            spread = jnp.broadcast_to(pooled_grad[plane][:, None], (10, 2, 16, 64))
            spread = spread.reshape(20, 16, 64)
            for half in range(2):
                at = 2 * (first + plane) + half
                seed = cd[6 + at, 6:26].astype(F32)
                grad = (seed + spread) * al[(6 + at) // 8, 6:26, :, 0:64]
                gw[at] = fine_window(grad).astype(BF)

    total = jnp.zeros((64, 1152), F32)
    for x in range(0, 16, 2):
        grad = gw[2 + x : 4 + x, 2:18].reshape(512, 128)[:, 32:96]
        taps = [
            fw[7 + x + tap // 3 : 9 + x + tap // 3, 7 + tap % 3 : 23 + tap % 3].reshape(512, 128)
            for tap in range(9)
        ]
        total = total + mm(grad, jnp.concatenate(taps, axis=1), TN)
    fine_scale = 1.0 / math.sqrt(524288)
    coarse_scale = 1.0 / math.sqrt(131072)
    sums[...] = jnp.zeros_like(sums)
    for tap in range(9):
        at = tap * 128
        term = total[0:32, at : at + 96] + total[32:64, at + 32 : at + 128]
        sums[0:32, tap * 96 : tap * 96 + 96] = term * fine_scale

    total = jnp.zeros((64, 1152), F32)
    total_up = jnp.zeros((128, 64), F32)
    for x in (0, 4):
        grad = cg[2 + x : 6 + x, 2:10].reshape(512, 256)[:, 64:128]
        taps = [
            pw[3 + x + tap // 3 : 7 + x + tap // 3, 3 + tap % 3 : 11 + tap % 3].reshape(512, 128)
            for tap in range(9)
        ]
        total = total + mm(grad, jnp.concatenate(taps, axis=1), TN)
        silu = act[2 + x : 6 + x, 2:10].reshape(512, 64)
        total_up = total_up + mm(gs[2 + x : 6 + x, 2:10].reshape(512, 128), silu, TN)
    for tap in range(9):
        at = tap * 128
        sums[32:96, tap * 96 : tap * 96 + 96] = total[:, at : at + 96] * coarse_scale
    total_up = total_up[0:32] + total_up[32:64] + total_up[64:96] + total_up[96:128]
    sums[0:32, 864:896] = total_up[:, 0:32] * coarse_scale
    sums[32:64, 864:896] = total_up[:, 32:64] * coarse_scale
    core = lax.axis_index("gy") % 2
    low, high = sums[0:48], sums[48:96]
    keep[...] = jnp.where(core == 0, low, high).astype(BF)
    send[...] = jnp.where(core == 0, high, low).astype(BF)


def to_bricks(meta, rows_of, ref):
    lane = lax.broadcasted_iota(jnp.int32, (256, 256), 1)
    row = lax.broadcasted_iota(jnp.int32, (256, 256), 0)
    same = (row >> 4) == ((lane & 127) >> 3)
    target = (row & 7) * 2 + ((row >> 3) & 1)
    even_lane = (lax.broadcasted_iota(jnp.int32, (32, 256), 1) & 1) == 0
    for cx in range(2):
        for cy in range(2):
            code = [meta_row(meta, 0, (cx * 2 + cy) * 2 + k) for k in range(2)]
            begin = jnp.concatenate([place(value) for value in code], axis=1)
            pick = (same & (((begin + (lane & 7)) >> 1) == target)).astype(F32).astype(BF)
            first = (cx * 2 + cy) * 64
            for g in range(4):
                rows = rows_of(cx * 8 + 2 * g, cy * 8)
                moved = mm(rows.reshape(256, 64), pick, TN)
                moved = jnp.where(even_lane, moved[0:32], moved[32:64]).astype(BF)
                cut = slice(g * 128, g * 128 + 128)
                ref[first : first + 32, cut] = moved[:, 0:128]
                ref[first + 32 : first + 64, cut] = moved[:, 128:256]


def finish_layer(fo, act, w_up, meta, out):
    twice = jnp.concatenate([w_up[...]] * 2, axis=0)
    up = mm(act[2:10, 2:10].reshape(1024, 64), twice, NT).reshape(8, 8, 16, 64)

    def rows_of(x, y):
        fine = fo[6 + x : 8 + x, y : y + 8].astype(F32)
        lifted = up[x // 2, y // 2 : 4 + y // 2]
        lifted = jnp.broadcast_to(lifted[:, None], (4, 2, 16, 64)).reshape(8, 16, 64)
        return (fine + lifted[None]).astype(BF)

    to_bricks(meta, rows_of, out)


def back_conv(first, gw, tb, back):
    for step in range(4):
        value = conv(gw, first + 1 + 2 * step, 2, 1, 16, tb)
        back[2 * step : 2 * step + 2] = value.astype(BF)


def finish_grad(low, high, meta, gfeat):
    def rows_of(x, y):
        ref = low if x < 8 else high
        return ref[x % 8 : x % 8 + 2, y : y + 8]

    to_bricks(meta, rows_of, gfeat)


def unpack(mine, other, gf, gc, gu):
    core = lax.axis_index("gy") % 2
    a, b = mine[...].astype(F32), other[...].astype(F32)
    low, high = jnp.where(core == 0, a, b), jnp.where(core == 0, b, a)
    gf[...] = low[0:32, 0:864]
    gc[0:16] = low[32:48, 0:864]
    gc[16:64] = high[:, 0:864]
    gu[:, 0:32] = low[0:32, 864:896]
    gu[0:16, 32:64] = low[32:48, 864:896]
    gu[16:32, 32:64] = high[0:16, 864:896]


def call(kernel, outs, scratch, args, mib, cost, far=False):
    whole = pl.BlockSpec(memory_space=pltpu.VMEM)
    anywhere = pl.BlockSpec(memory_space=pltpu.HBM)
    return pl.pallas_call(
        kernel,
        out_shape=tuple(jax.ShapeDtypeStruct(shape, kind) for shape, kind in outs),
        in_specs=[anywhere if far else whole] * len(args),
        out_specs=(whole,) * len(outs),
        scratch_shapes=scratch if far else [pltpu.VMEM(shape, kind) for shape, kind in scratch],
        compiler_params=pltpu.CompilerParams(vmem_limit_bytes=mib * 1024 * 1024),
        cost_estimate=pl.CostEstimate(flops=cost, bytes_accessed=2000000, transcendentals=0),
    )(*args)


def swap_pairs(length, first):
    pairs = []
    for i in range(first, length - 1, 2):
        pairs += [(i, i + 1), (i + 1, i)]
    return pairs


def core_pairs(total):
    return [(i, i ^ 1) for i in range(total)]


def ring_pairs(total, shifts, across):
    pairs = []
    for i in range(total):
        shift = shifts[i & 1]
        q = (i >> shift) & 3
        mate = (q + 1 if q % 2 else q - 1) % 4 if across else q ^ 1
        pairs.append((i, (i & ~(3 << shift)) | (mate << shift)))
    return pairs


def local(features, w_fine, w_coarse, w_up, cotangent, adjacency, parents):
    wide, across = lax.axis_size("gx"), lax.axis_size("gy")
    total = wide * across
    feat = features.reshape(256, 512)
    cot = cotangent.reshape(256, 512)
    first, second, first_y, second_y, own = call(
        pack_own,
        [((784, 128), BF)] * 4 + [((720, 512), BF)],
        [
            pltpu.VMEM((32, 864), BF),
            pltpu.VMEM((64, 864), BF),
            pltpu.SMEM((8,), jnp.int32),
            pltpu.SemaphoreType.DMA((5,)),
        ],
        (parents, feat, cot, w_fine, w_coarse), 62, 1000000, far=True,
    )
    xa = lax.ppermute(first, "gx", swap_pairs(wide, 0))
    xb = lax.ppermute(second, "gx", swap_pairs(wide, 1))
    oa = lax.ppermute(first_y, "gy", swap_pairs(across, 0))
    ob = lax.ppermute(second_y, "gy", swap_pairs(across, 1))
    own_fw, own_cd, tf, tb, tc, tg, in_fo, in_pw, meta = call(
        prepare,
        [((16, 16, 16, 128), BF), ((16, 16, 16, 64), BF)]
        + [((384, 192), BF)] * 3
        + [((768, 192), BF), ((12, 12, 16, 64), BF), ((6, 6, 16, 128), BF), ((16, 128), BF)],
        [((192, 384), F32), ((192, 384), F32), ((2, 16, 16, 128), F32)],
        (own,), 12, 4000000000,
    )
    first, second = call(
        pack_corners, [((672, 128), BF), ((672, 128), BF)], [], (xa, xb), 6, 1000000,
    )
    ya = lax.ppermute(first, "gy", swap_pairs(across, 0))
    yb = lax.ppermute(second, "gy", swap_pairs(across, 1))
    mid_fw, mid_cd, mid_fo, mid_pw = call(
        middle,
        [((32, 32, 16, 128), BF), ((32, 32, 16, 64), BF),
         ((16, 12, 16, 64), BF), ((8, 6, 16, 128), BF)],
        [((4, 16, 16, 128), F32)],
        (xa, xb, oa, ob, meta, own_fw, own_cd, tf), 20, 6000000000,
    )
    gw, fo, act, keep, send = call(
        main,
        [((20, 20, 16, 128), BF), ((28, 16, 16, 64), BF), ((12, 12, 16, 64), BF),
         ((48, 896), BF), ((48, 896), BF)],
        [
            ((32, 32, 16, 128), BF),
            ((32, 32, 16, 64), BF),
            ((4, 32, 16, 128), F32),
            ((16, 16, 16, 128), BF),
            ((12, 12, 16, 256), BF),
            ((12, 12, 16, 128), BF),
            ((96, 896), F32),
        ],
        (xa, xb, oa, ob, ya, yb, meta, mid_fw, mid_cd, mid_fo, mid_pw, in_fo, in_pw, tf, tc, tg, w_up),
        36, 20000000000,
    )

    def layer_part(args):
        return call(finish_layer, [((256, 512), BF)], [], args, 8, 2000000000)

    def back_part(first):
        def part(args):
            kernel = functools.partial(back_conv, first)
            return call(kernel, [((8, 16, 16, 64), BF)], [], args, 8, 2000000000)

        return part

    def grad_part(args):
        return call(finish_grad, [((256, 512), BF)], [], args, 8, 2000000000)

    def add(value, pairs, sent=None, part=None, args=()):
        value, args = lax.optimization_barrier((value, args)) if part else (value, args)
        other = lax.ppermute(value if sent is None else sent, AXES, pairs)
        done = part(args)[0] if part else None
        value = (value.astype(F32) + other.astype(F32)).astype(BF)
        return lax.optimization_barrier((value, done)) if part else (value, None)

    value, _ = add(keep, core_pairs(total), send)
    value, out = add(value, ring_pairs(total, (1, 3), False), None, layer_part, (fo, act, w_up, meta))
    value, low = add(value, ring_pairs(total, (1, 3), True), None, back_part(0), (gw, tb))
    value, high = add(value, ring_pairs(total, (3, 5), False), None, back_part(8), (gw, tb))
    value, gfeat = add(value, ring_pairs(total, (3, 5), True), None, grad_part, (low, high, meta))
    value, _ = add(value, ring_pairs(total, (5, 1), False))
    value, _ = add(value, ring_pairs(total, (5, 1), True))
    other = lax.ppermute(value, AXES, core_pairs(total))
    gf, gc, gu = call(
        unpack, [((32, 864), F32), ((64, 864), F32), ((32, 64), F32)], [], (value, other), 4, 1000000
    )
    return out.reshape(features.shape), gfeat.reshape(features.shape), gf, gc, gu


def solution(mesh):
    return jax.shard_map(
        local,
        mesh=mesh,
        in_specs=(
            P(("gx", "gy"), None, None),
            P(),
            P(),
            P(),
            P(("gx", "gy"), None, None),
            P(("gx", "gy"), None),
            P(("gx", "gy")),
        ),
        out_specs=(P(("gx", "gy"), None, None), P(("gx", "gy"), None, None), P(), P(), P()),
        check_vma=False,
    )
```

```python
import functools
import math

import jax
import jax.numpy as jnp
from jax import lax
from jax.experimental import pallas as pl
from jax.experimental.pallas import tpu as pltpu
from jax.sharding import PartitionSpec as P

BF = jnp.bfloat16
F32 = jnp.float32
AXES = ("gx", "gy")
NN = (((1,), (0,)), ((), ()))
NT = (((1,), (1,)), ((), ()))
TN = (((0,), (0,)), ((), ()))


def mm(a, b, dims=NN):
    return lax.dot_general(a, b, dims, preferred_element_type=F32)


def halves(value):
    even, odd = value[:, 0:8], value[:, 8:16]
    blank = jnp.zeros((value.shape[0], 1, value.shape[2]), value.dtype)
    odd_before = jnp.concatenate([blank, odd[:, 0:7]], axis=1)
    even_after = jnp.concatenate([even[:, 1:8], blank], axis=1)
    return even, odd, odd_before, even_after


def coarse_window(value):
    even, odd, odd_before, even_after = halves(value)
    blank = jnp.zeros_like(even)
    top = jnp.concatenate([odd_before, even, odd, blank], axis=2)
    low = jnp.concatenate([even, odd, even_after, blank], axis=2)
    return jnp.concatenate([top, low], axis=1)


def fine_window(value):
    even, odd, odd_before, even_after = halves(value)
    top = jnp.concatenate([odd_before[:, :, 32:64], even, odd[:, :, 0:32]], axis=2)
    low = jnp.concatenate([even[:, :, 32:64], odd, even_after[:, :, 0:32]], axis=2)
    return jnp.concatenate([top, low], axis=1)


def place(code):
    return jnp.where(code > 0, code.astype(jnp.int32) * 8 - 8, -100)


def meta_row(ref, base, slot):
    return ref[base : base + 16, 0:128].astype(F32)[slot : slot + 1]


class Either:
    def __init__(self, flag, first, second):
        self.flag, self.first, self.second = flag, first, second

    def __getitem__(self, index):
        return jnp.where(self.flag, self.first[index], self.second[index])


def sides(axis, first, second):
    even = lax.axis_index(axis) % 2 == 0
    return Either(even, second, first), Either(even, first, second)


def by_swap(axis, write, first, second):
    even = lax.axis_index(axis) % 2 == 0

    @pl.when(even)
    def _():
        write(first, second)

    @pl.when(jnp.logical_not(even))
    def _():
        write(second, first)


def roll(value, by):
    return pltpu.roll(value.astype(F32), by, 1).astype(BF)


def source(cx, cy, refs):
    if cy in (1, 2) and cx in (1, 2):
        (own,) = refs
        first = ((cx - 1) * 2 + cy - 1) * 2

        def cut(base, k, g):
            at = base + (first + k) * 32
            return own[at : at + 32, g * 128 : g * 128 + 128]

        return (
            lambda k, g: cut(0, k, g),
            lambda k, g: cut(256, k, g),
            [meta_row(own, 512, first + k) for k in range(2)],
        )
    (ref,) = refs
    if cy in (1, 2):
        first = (cy - 1) * 2
        sender = ((1 if cx == 0 else 0) * 2 + cy - 1) * 2

        def features(k, g):
            at = ((first + k) * 4 + g) * 32
            return ref[at : at + 32]

        def cotangents(k, g):
            at = 512 + ((first + k) * 2 + g % 2) * 32
            return ref[at : at + 32]

        return features, cotangents, [meta_row(ref, 768, sender + k) for k in range(2)]
    sender = ((1, 0, 1, 0)[cx] * 2 + (1 if cy == 0 else 0)) * 2
    corner = cx in (0, 3)
    place_in = cx // 3 if corner else cx - 1
    base = 640 + place_in * 16 if corner else 768

    def features(k, g):
        at = ((place_in * 2 + k) * 4 + g) * 32
        return ref[at : at + 32]

    def cotangents(k, g):
        at = 512 + ((place_in if corner else place_in * 2 + g // 2) * 2 + k) * 32
        packed = ref[at : at + 32]
        return packed if g % 2 == 0 else roll(packed, 32 if cy == 0 else 96)

    return features, cotangents, [meta_row(ref, base, sender + k) for k in range(2)]


def half_rows(side, here, there):
    high = (lax.broadcasted_iota(jnp.int32, (32, 128), 1) & 32) != 0
    if side == 1:
        return jnp.where(high, here, roll(there, 96))
    return jnp.where(high, roll(there, 32), here)


def live_rows(code):
    pair = lax.broadcasted_iota(jnp.int32, (16, 128), 0)
    pair = (pair & 7) * 2 + (pair >> 3)
    live = jnp.zeros((16, 128), F32)
    for value in code:
        live = live + ((pair >> 2) == (value.astype(jnp.int32) - 1)).astype(F32)
    return live


def place_column(cx, cy, refs, fw, cd, x_at, y_at):
    features, cotangents, code = source(cx, cy, refs)
    lane = lax.broadcasted_iota(jnp.int32, (128, 256), 1)
    row = lax.broadcasted_iota(jnp.int32, (128, 256), 0)
    same = (row >> 3) == ((lane & 127) >> 3)
    res = lax.broadcasted_iota(jnp.int32, (32, 256), 1) & 3
    begin = jnp.concatenate([place(value) for value in code], axis=1)
    shift = begin + (lane & 7) - ((row & 7) * 4 - 1)
    pick_even = (same & (shift >= 0) & (shift < 4)).astype(F32).astype(BF)
    pick_odd = (same & (shift >= 2) & (shift < 6)).astype(F32).astype(BF)
    wanted = {0: (2, 3), 1: (0, 1, 2, 3), 2: (0, 1, 2, 3), 3: (0, 1)}[cx]
    for g in range(4):
        f = jnp.concatenate([features(k, g) for k in range(2)], axis=1)
        none = jnp.zeros_like(f)
        fr = [jnp.where(res == i, f, none) for i in range(4)]
        even, odd = [fr[3], fr[0], fr[1], fr[2]], [fr[1], fr[2], fr[3], fr[0]]
        if g in wanted:
            c = jnp.concatenate([cotangents(k, g) for k in range(2)], axis=1)
            cr = [jnp.where(res == i, c, none) for i in range(4)]
            even, odd = even + cr[0:2], odd + cr[2:4]
        lanes = 32 * len(even)
        even = mm(pick_even, jnp.concatenate(even, axis=0), NT).reshape(16, 8, lanes)
        odd = mm(pick_odd, jnp.concatenate(odd, axis=0), NT).reshape(16, 8, lanes)
        both = jnp.concatenate([even, odd], axis=1)
        xs = slice(x_at + 2 * g, x_at + 2 * g + 2)
        ys = slice(y_at, y_at + 8)
        fw[xs, ys] = both[:, :, 0:128].astype(BF).reshape(2, 8, 16, 128)
        if g in wanted:
            cd[xs, ys] = both[:, :, 128:192].astype(BF).reshape(2, 8, 16, 64)
    return code


def pack_own(
    parents_far, feat_far, cot_far, w_fine_far, w_coarse_far,
    first, second, first_y, second_y, own, w_fine, w_coarse, parents, sems,
):
    copies = [
        pltpu.make_async_copy(source_ref, target, sems.at[i])
        for i, (source_ref, target) in enumerate(
            (
                (parents_far, parents),
                (feat_far, own.at[0:256]),
                (cot_far, own.at[256:512]),
                (w_fine_far, w_fine),
                (w_coarse_far, w_coarse),
            )
        )
    ]
    for copy in copies:
        copy.start()
    copies[0].wait()
    row = lax.broadcasted_iota(jnp.int32, (16, 128), 0)
    code = jnp.zeros((16, 128), F32)
    for slot in range(8):
        value = parents[slot]
        depth = jnp.where(value >= 0, ((value >> 3) & 1) * 2 + (value & 1) + 1, 0)
        code = jnp.where(row == slot, depth.astype(F32), code)
    code = code.astype(BF)
    own[512:528] = jnp.concatenate([code] * 4, axis=1)
    copies[1].wait()
    copies[2].wait()

    def write(up, down):
        for ref, side in ((up, 1), (down, 0)):
            for slot in range(4):
                at = (side * 4 + slot) * 32
                for g in range(4):
                    to = (slot * 4 + g) * 32
                    ref[to : to + 32] = own[at : at + 32, g * 128 : g * 128 + 128]
                for part in range(2):
                    to = 512 + (slot * 2 + part) * 32
                    lanes = slice((2 * side + part) * 128, (2 * side + part) * 128 + 128)
                    ref[to : to + 32] = own[256 + at : 288 + at, lanes]
            ref[768:784] = code

    def write_y(up, down):
        for ref, side in ((up, 1), (down, 0)):
            for cx in (1, 2):
                features, cotangents, _ = source(cx, side + 1, (own,))
                for k in range(2):
                    for g in range(4):
                        to = (((cx - 1) * 2 + k) * 4 + g) * 32
                        ref[to : to + 32] = features(k, g)
                    for g in (0, 2):
                        to = 512 + (((cx - 1) * 2 + g // 2) * 2 + k) * 32
                        ref[to : to + 32] = half_rows(side, cotangents(k, g), cotangents(k, g + 1))
            ref[768:784] = code

    by_swap("gx", write, first, second)
    by_swap("gy", write_y, first_y, second_y)
    for copy in copies[3:]:
        copy.wait()
    for ref, at in ((w_fine, 528), (w_coarse, 560)):
        rows = ref.shape[0]
        own[at : at + rows] = ref[:, 0:512]
        own[at + 96 : at + 96 + rows, 0:352] = ref[:, 512:864]


def pack_corners(xa, xb, first, second):
    xm, xp = sides("gx", xa, xb)

    def write(up, down):
        for ref, side in ((up, 1), (down, 0)):
            for at, (cx, came) in enumerate(((0, xm), (3, xp))):
                features, cotangents, _ = source(cx, side + 1, (came,))
                for k in range(2):
                    for g in range(4):
                        to = ((at * 2 + k) * 4 + g) * 32
                        ref[to : to + 32] = features(k, g)
                    to = 512 + (at * 2 + k) * 32
                    ref[to : to + 32] = half_rows(side, cotangents(k, 0), cotangents(k, 1))
                ref[640 + at * 16 : 656 + at * 16] = came[768:784]

    by_swap("gy", write, first, second)


def prepare(
    own,
    fw, cd, tf, tc, tg, fo, pw, meta,
    turned_f, turned_c, al,
):
    w_fine = jnp.concatenate([own[528:560], own[624:656, 0:352]], axis=1)
    w_coarse = jnp.concatenate([own[560:624], own[656:720, 0:352]], axis=1)
    meta[...] = own[512:528, 0:128]
    turned_f[...] = jnp.zeros_like(turned_f)
    turned_c[...] = jnp.zeros_like(turned_c)
    tg[...] = jnp.zeros_like(tg)
    for tx in range(3):
        for ty in range(3):
            at = (tx * 3 + ty) * 96
            for zo in range(2):
                to, lanes = (ty * 2 + zo) * 32, tx * 128 + zo * 32
                turned_f[to : to + 32, lanes : lanes + 96] = w_fine[:, at : at + 96].astype(F32)
            turned_c[ty * 64 : ty * 64 + 64, tx * 128 : tx * 128 + 96] = w_coarse[
                :, at : at + 96
            ].astype(F32)
            for tz in range(3):
                at = (((2 - tx) * 3 + 2 - ty) * 3 + 2 - tz) * 32
                for zo in range(2):
                    lanes = (ty * 2 + zo) * 32
                    to = tx * 256 + tz * 64
                    tg[to : to + 64, lanes : lanes + 32] = w_coarse[:, at : at + 32]
    row = lax.broadcasted_iota(jnp.int32, (384, 384), 0)
    eye = (row == lax.broadcasted_iota(jnp.int32, (384, 384), 1)).astype(F32).astype(BF)
    tf[...] = mm(eye, turned_f[...].astype(BF), NT).astype(BF)
    tc[...] = mm(eye, turned_c[...].astype(BF), NT).astype(BF)
    for cx in (1, 2):
        for cy in (1, 2):
            code = place_column(cx, cy, (own,), fw, cd, cx * 8 - 8, cy * 8 - 8)
            live = live_rows(code)
            for y in range(8):
                al[cx - 1, cy * 8 - 8 + y] = live
    for at in range(6):
        value = conv(fw, 1 + 2 * at, 2, 1, 12, tf)
        fine = (value * al[(2 + 2 * at) // 8, 2:14, :, 0:64][None]).astype(BF)
        pw[at] = pool(fine)
        fo[2 * at : 2 * at + 2] = fine


def conv_rows(ref, x_first, planes, y_first, width):
    rows = planes * (width + 2) * 16
    return jnp.concatenate(
        [
            ref[pl.ds(x_first + tap, planes), y_first : y_first + width + 2].reshape(
                rows, ref.shape[3]
            )
            for tap in range(3)
        ],
        axis=1,
    )


def conv_taps(wide, width):
    return (
        wide[:, 0:width, :, 0:64]
        + wide[:, 1 : width + 1, :, 64:128]
        + wide[:, 2 : width + 2, :, 128:192]
    )


def conv(ref, x_first, planes, y_first, width, weight):
    rows = conv_rows(ref, x_first, planes, y_first, width)
    return conv_taps(mm(rows, weight[...]).reshape(planes, width + 2, 16, 192), width)


def pool(fine):
    rows = fine.shape[1] // 2
    pooled = fine.astype(F32)
    pooled = (pooled[0] + pooled[1]).reshape(rows, 2, 16, 64)
    pooled = pooled[:, 0] + pooled[:, 1]
    return coarse_window((pooled[:, :, 0:32] + pooled[:, :, 32:64]) * 0.125).astype(BF)


def middle(xa, xb, oa, ob, meta, own_fw, own_cd, tf, fw, cd, fo, pw, al):
    xm, xp = sides("gx", xa, xb)
    om, op = sides("gy", oa, ob)
    fw[8:24, 8:24] = own_fw[...]
    cd[8:24, 8:24] = own_cd[...]
    for cx in (1, 2):
        place_column(cx, 0, (om,), fw, cd, cx * 8, 0)
        place_column(cx, 3, (op,), fw, cd, cx * 8, 24)
    for cx in range(4):
        for cy in (1, 2):
            if cx in (0, 3):
                refs = (xm,) if cx == 0 else (xp,)
                code = place_column(cx, cy, refs, fw, cd, cx * 8, cy * 8)
            else:
                code = [meta_row(meta, 0, ((cx - 1) * 2 + cy - 1) * 2 + k) for k in range(2)]
            live = live_rows(code)
            for y in range(8):
                al[cx, cy * 8 - 8 + y] = live

    for order, at in enumerate((0, 1, 2, 3, 10, 11, 12, 13)):
        value = conv(fw, 1 + 2 * at, 2, 9, 12, tf)
        fine = (value * al[(2 + 2 * at) // 8, 2:14, :, 0:64][None]).astype(BF)
        pw[order] = pool(fine)
        fo[2 * order : 2 * order + 2] = fine


def main(
    xa, xb, oa, ob, ya, yb, meta, mid_fw, mid_cd, mid_fo, mid_pw, in_fo, in_pw, tf, tc, tg, w_up,
    gw, fo, act, keep, send,
    fw, cd, al, pw, cg, gs, sums,
):
    xm, xp = sides("gx", xa, xb)
    om, op = sides("gy", oa, ob)
    ym, yp = sides("gy", ya, yb)
    for ref, came, rim in ((fw, mid_fw, 1), (cd, mid_cd, 4)):
        ref[rim : 32 - rim, 8:24] = came[rim : 32 - rim, 8:24]
        ref[8:24, rim:8] = came[8:24, rim:8]
        ref[8:24, 24 : 32 - rim] = came[8:24, 24 : 32 - rim]
    fo[0:8, 2:14] = mid_fo[0:8]
    fo[8:20, 2:14] = in_fo[...]
    fo[20:28, 2:14] = mid_fo[8:16]
    pw[1:5, 5:11] = mid_pw[0:4]
    pw[5:11, 5:11] = in_pw[...]
    pw[11:15, 5:11] = mid_pw[4:8]
    for cx in range(4):
        for cy in range(4):
            if cy in (0, 3):
                if cx in (0, 3):
                    refs = (ym,) if cy == 0 else (yp,)
                    code = place_column(cx, cy, refs, fw, cd, cx * 8, cy * 8)
                else:
                    code = source(cx, cy, (om,) if cy == 0 else (op,))[2]
            else:
                if cx in (0, 3):
                    code = source(cx, cy, (xm,) if cx == 0 else (xp,))[2]
                else:
                    code = [meta_row(meta, 0, ((cx - 1) * 2 + cy - 1) * 2 + k) for k in range(2)]
            live = live_rows(code)
            for y in range(8):
                al[cx, cy * 8 + y] = live

    for step in range(14):
        rows = [conv_rows(fw, 1 + 2 * step, 2, first, 8) for first in (1, 21)]
        wide = mm(jnp.concatenate(rows, axis=0), tf[...]).reshape(2, 2, 10, 16, 192)
        column = (2 + 2 * step) // 8
        first = (conv_taps(wide[0], 8) * al[column, 2:10, :, 0:64][None]).astype(BF)
        second = (conv_taps(wide[1], 8) * al[column, 22:30, :, 0:64][None]).astype(BF)
        pw[1 + step, 1:5] = pool(first)
        pw[1 + step, 11:15] = pool(second)
        fo[2 * step : 2 * step + 2, 0:2] = first[:, 6:8]
        fo[2 * step : 2 * step + 2, 14:16] = second[:, 0:2]

    four = jnp.concatenate([w_up[...]] * 4, axis=0)
    for x in range(0, 12, 4):
        pre = conv(pw, 1 + x, 4, 1, 12, tc)
        sig = 1.0 / (1.0 + jnp.exp(-pre))
        act[x : x + 4] = (pre * sig).astype(BF)
        pair = cd[4 + 2 * x : 4 + 2 * x + 2 * 4, 4:28].astype(F32).reshape(4, 2, 24, 16, 64)
        pair = (pair[:, 0] + pair[:, 1]).reshape(4, 12, 2, 16, 64)
        pair = pair[:, :, 0] + pair[:, :, 1]
        high = pair.astype(BF)
        low = (pair - high.astype(F32)).astype(BF)
        split = jnp.concatenate([high, low], axis=3)
        gs[x : x + 4] = split
        back = mm(split.reshape(4 * 192, 128), four).reshape(4, 12, 16, 64)
        grad = back * sig * (1.0 + pre * (1.0 - sig))
        window = coarse_window(grad.reshape(4 * 12, 16, 64)).astype(BF)
        cg[x : x + 4] = window.reshape(4, 12, 16, 256)

    for first in range(0, 10, 1):
        pooled_grad = conv(cg, first, 1, 0, 10, tg) * 0.125
        for plane in range(1):
            spread = jnp.broadcast_to(pooled_grad[plane][:, None], (10, 2, 16, 64))
            spread = spread.reshape(20, 16, 64)
            for half in range(2):
                at = 2 * (first + plane) + half
                seed = cd[6 + at, 6:26].astype(F32)
                grad = (seed + spread) * al[(6 + at) // 8, 6:26, :, 0:64]
                gw[at] = fine_window(grad).astype(BF)

    total = jnp.zeros((64, 1152), F32)
    for x in range(0, 16, 2):
        grad = gw[2 + x : 4 + x, 2:18].reshape(512, 128)[:, 32:96]
        taps = [
            fw[7 + x + tap // 3 : 9 + x + tap // 3, 7 + tap % 3 : 23 + tap % 3].reshape(512, 128)
            for tap in range(9)
        ]
        total = total + mm(grad, jnp.concatenate(taps, axis=1), TN)
    fine_scale = 1.0 / math.sqrt(524288)
    coarse_scale = 1.0 / math.sqrt(131072)
    sums[64:96, 864:896] = jnp.zeros((32, 32), F32)
    for tap in range(9):
        at = tap * 128
        term = total[0:32, at : at + 96] + total[32:64, at + 32 : at + 128]
        sums[0:32, tap * 96 : tap * 96 + 96] = term * fine_scale

    total = jnp.zeros((64, 1152), F32)
    total_up = jnp.zeros((128, 64), F32)
    for x in (0, 4):
        grad = cg[2 + x : 6 + x, 2:10].reshape(512, 256)[:, 64:128]
        taps = [
            pw[3 + x + tap // 3 : 7 + x + tap // 3, 3 + tap % 3 : 11 + tap % 3].reshape(512, 128)
            for tap in range(9)
        ]
        total = total + mm(grad, jnp.concatenate(taps, axis=1), TN)
        silu = act[2 + x : 6 + x, 2:10].reshape(512, 64)
        total_up = total_up + mm(gs[2 + x : 6 + x, 2:10].reshape(512, 128), silu, TN)
    for tap in range(9):
        at = tap * 128
        sums[32:96, tap * 96 : tap * 96 + 96] = total[:, at : at + 96] * coarse_scale
    total_up = total_up[0:32] + total_up[32:64] + total_up[64:96] + total_up[96:128]
    sums[0:32, 864:896] = total_up[:, 0:32] * coarse_scale
    sums[32:64, 864:896] = total_up[:, 32:64] * coarse_scale
    core = lax.axis_index("gy") % 2
    low, high = sums[0:48], sums[48:96]
    keep[...] = jnp.where(core == 0, low, high).astype(BF)
    send[...] = jnp.where(core == 0, high, low).astype(BF)


def to_bricks(meta, rows_of, ref):
    lane = lax.broadcasted_iota(jnp.int32, (256, 256), 1)
    row = lax.broadcasted_iota(jnp.int32, (256, 256), 0)
    same = (row >> 4) == ((lane & 127) >> 3)
    target = (row & 7) * 2 + ((row >> 3) & 1)
    even_lane = (lax.broadcasted_iota(jnp.int32, (32, 256), 1) & 1) == 0
    for cx in range(2):
        for cy in range(2):
            code = [meta_row(meta, 0, (cx * 2 + cy) * 2 + k) for k in range(2)]
            begin = jnp.concatenate([place(value) for value in code], axis=1)
            pick = (same & (((begin + (lane & 7)) >> 1) == target)).astype(F32).astype(BF)
            first = (cx * 2 + cy) * 64
            for g in range(4):
                rows = rows_of(cx * 8 + 2 * g, cy * 8)
                moved = mm(rows.reshape(256, 64), pick, TN)
                moved = jnp.where(even_lane, moved[0:32], moved[32:64]).astype(BF)
                cut = slice(g * 128, g * 128 + 128)
                ref[first : first + 32, cut] = moved[:, 0:128]
                ref[first + 32 : first + 64, cut] = moved[:, 128:256]


def finish_layer(fo, act, w_up, meta, own, out, tb):
    w_fine = jnp.concatenate([own[528:560], own[624:656, 0:352]], axis=1)
    tb[...] = jnp.zeros_like(tb)
    for tap in range(27):
        tx, ty, tz = tap // 9, tap // 3 % 3, tap % 3
        at = (26 - tap) * 32
        for zo in range(2):
            lanes = (ty * 2 + zo) * 32
            to = tx * 128 + (tz + zo) * 32
            tb[to : to + 32, lanes : lanes + 32] = w_fine[:, at : at + 32]
    twice = jnp.concatenate([w_up[...]] * 2, axis=0)
    up = mm(act[2:10, 2:10].reshape(1024, 64), twice, NT).reshape(8, 8, 16, 64)

    def rows_of(x, y):
        fine = fo[6 + x : 8 + x, y : y + 8].astype(F32)
        lifted = up[x // 2, y // 2 : 4 + y // 2]
        lifted = jnp.broadcast_to(lifted[:, None], (4, 2, 16, 64)).reshape(8, 16, 64)
        return (fine + lifted[None]).astype(BF)

    to_bricks(meta, rows_of, out)


def back_conv(first, gw, tb, back):
    for step in range(4):
        value = conv(gw, first + 1 + 2 * step, 2, 1, 16, tb)
        back[2 * step : 2 * step + 2] = value.astype(BF)


def finish_grad(low, high, meta, gfeat):
    def rows_of(x, y):
        ref = low if x < 8 else high
        return ref[x % 8 : x % 8 + 2, y : y + 8]

    to_bricks(meta, rows_of, gfeat)


def unpack(mine, other, gf, gc, gu):
    core = lax.axis_index("gy") % 2
    a, b = mine[...].astype(F32), other[...].astype(F32)
    low, high = jnp.where(core == 0, a, b), jnp.where(core == 0, b, a)
    gf[...] = low[0:32, 0:864]
    gc[0:16] = low[32:48, 0:864]
    gc[16:64] = high[:, 0:864]
    gu[:, 0:32] = low[0:32, 864:896]
    gu[0:16, 32:64] = low[32:48, 864:896]
    gu[16:32, 32:64] = high[0:16, 864:896]


def call(kernel, outs, scratch, args, mib, cost, far=False):
    whole = pl.BlockSpec(memory_space=pltpu.VMEM)
    anywhere = pl.BlockSpec(memory_space=pltpu.HBM)
    return pl.pallas_call(
        kernel,
        out_shape=tuple(jax.ShapeDtypeStruct(shape, kind) for shape, kind in outs),
        in_specs=[anywhere if far else whole] * len(args),
        out_specs=(whole,) * len(outs),
        scratch_shapes=scratch if far else [pltpu.VMEM(shape, kind) for shape, kind in scratch],
        compiler_params=pltpu.CompilerParams(vmem_limit_bytes=mib * 1024 * 1024),
        cost_estimate=pl.CostEstimate(flops=cost, bytes_accessed=2000000, transcendentals=0),
    )(*args)


def swap_pairs(length, first):
    pairs = []
    for i in range(first, length - 1, 2):
        pairs += [(i, i + 1), (i + 1, i)]
    return pairs


def core_pairs(total):
    return [(i, i ^ 1) for i in range(total)]


def ring_pairs(total, shifts, across):
    pairs = []
    for i in range(total):
        shift = shifts[i & 1]
        q = (i >> shift) & 3
        mate = (q + 1 if q % 2 else q - 1) % 4 if across else q ^ 1
        pairs.append((i, (i & ~(3 << shift)) | (mate << shift)))
    return pairs


def local(features, w_fine, w_coarse, w_up, cotangent, adjacency, parents):
    wide, across = lax.axis_size("gx"), lax.axis_size("gy")
    total = wide * across
    feat = features.reshape(256, 512)
    cot = cotangent.reshape(256, 512)
    first, second, first_y, second_y, own = call(
        pack_own,
        [((784, 128), BF)] * 4 + [((720, 512), BF)],
        [
            pltpu.VMEM((32, 864), BF),
            pltpu.VMEM((64, 864), BF),
            pltpu.SMEM((8,), jnp.int32),
            pltpu.SemaphoreType.DMA((5,)),
        ],
        (parents, feat, cot, w_fine, w_coarse), 62, 1000000, far=True,
    )
    oa = lax.ppermute(first_y, "gy", swap_pairs(across, 0))
    ob = lax.ppermute(second_y, "gy", swap_pairs(across, 1))
    xa = lax.ppermute(first, "gx", swap_pairs(wide, 0))
    xb = lax.ppermute(second, "gx", swap_pairs(wide, 1))
    own_fw, own_cd, tf, tc, tg, in_fo, in_pw, meta = call(
        prepare,
        [((16, 16, 16, 128), BF), ((16, 16, 16, 64), BF)]
        + [((384, 192), BF)] * 2
        + [((768, 192), BF), ((12, 12, 16, 64), BF), ((6, 6, 16, 128), BF), ((16, 128), BF)],
        [((192, 384), F32), ((192, 384), F32), ((2, 16, 16, 128), F32)],
        (own,), 12, 4000000000,
    )
    first, second = call(
        pack_corners, [((672, 128), BF), ((672, 128), BF)], [], (xa, xb), 6, 1000000,
    )
    ya = lax.ppermute(first, "gy", swap_pairs(across, 0))
    yb = lax.ppermute(second, "gy", swap_pairs(across, 1))
    mid_fw, mid_cd, mid_fo, mid_pw = call(
        middle,
        [((32, 32, 16, 128), BF), ((32, 32, 16, 64), BF),
         ((16, 12, 16, 64), BF), ((8, 6, 16, 128), BF)],
        [((4, 16, 16, 128), F32)],
        (xa, xb, oa, ob, meta, own_fw, own_cd, tf), 20, 6000000000,
    )
    gw, fo, act, keep, send = call(
        main,
        [((20, 20, 16, 128), BF), ((28, 16, 16, 64), BF), ((12, 12, 16, 64), BF),
         ((48, 896), BF), ((48, 896), BF)],
        [
            ((32, 32, 16, 128), BF),
            ((32, 32, 16, 64), BF),
            ((4, 32, 16, 128), F32),
            ((16, 16, 16, 128), BF),
            ((12, 12, 16, 256), BF),
            ((12, 12, 16, 128), BF),
            ((96, 896), F32),
        ],
        (xa, xb, oa, ob, ya, yb, meta, mid_fw, mid_cd, mid_fo, mid_pw, in_fo, in_pw, tf, tc, tg, w_up),
        36, 20000000000,
    )

    def layer_part(args):
        return call(
            finish_layer, [((256, 512), BF), ((384, 192), BF)], [], args, 10, 2000000000
        )

    def back_part(first):
        def part(args):
            kernel = functools.partial(back_conv, first)
            return call(kernel, [((8, 16, 16, 64), BF)], [], args, 8, 2000000000)

        return part

    def grad_part(args):
        return call(finish_grad, [((256, 512), BF)], [], args, 8, 2000000000)

    def add(value, pairs, sent=None, part=None, args=()):
        value, args = lax.optimization_barrier((value, args)) if part else (value, args)
        other = lax.ppermute(value if sent is None else sent, AXES, pairs)
        done = part(args) if part else None
        value = (value.astype(F32) + other.astype(F32)).astype(BF)
        return lax.optimization_barrier((value, done)) if part else (value, None)

    value, _ = add(keep, core_pairs(total), send)
    value, (out, tb) = add(value, ring_pairs(total, (3, 5), False), None, layer_part, (fo, act, w_up, meta, own))
    value, (low,) = add(value, ring_pairs(total, (3, 5), True), None, back_part(0), (gw, tb))
    value, (high,) = add(value, ring_pairs(total, (1, 3), False), None, back_part(8), (gw, tb))
    value, (gfeat,) = add(value, ring_pairs(total, (1, 3), True), None, grad_part, (low, high, meta))
    value, _ = add(value, ring_pairs(total, (5, 1), False))
    value, _ = add(value, ring_pairs(total, (5, 1), True))
    other = lax.ppermute(value, AXES, core_pairs(total))
    gf, gc, gu = call(
        unpack, [((32, 864), F32), ((64, 864), F32), ((32, 64), F32)], [], (value, other), 4, 1000000
    )
    return out.reshape(features.shape), gfeat.reshape(features.shape), gf, gc, gu


def solution(mesh):
    return jax.shard_map(
        local,
        mesh=mesh,
        in_specs=(
            P(("gx", "gy"), None, None),
            P(),
            P(),
            P(),
            P(("gx", "gy"), None, None),
            P(("gx", "gy"), None),
            P(("gx", "gy")),
        ),
        out_specs=(P(("gx", "gy"), None, None), P(("gx", "gy"), None, None), P(), P(), P()),
        check_vma=False,
    )
```
